32 devices in a mesh: gx: 4 (over y, core), gy: 8 (over z, x).
Axes of the slice: x: 2, y: 2, z: 4, core: 2. Of those that a mesh axis runs over, the one named last changes fastest.
Arguments:
- tensor: float32 [2048, 1024, 32], P('gx', 'gy'), may hold values from -6 to 6
- factor_two: float32 [1024, 64], P('gy', 'gx'), may hold values from -0.1875 to 0.1875
- factor_three: float32 [32, 64], replicated, may hold values from -1 to 1
Outputs:
- factor_one: float32 [2048, 64], P(('gx', 'gy'))
The draws below stay inside these ranges and needn't reach their ends.
All inputs are finite; a program needn't handle non-finite values.
Results may differ from the reference program's by a relative error of at most 0.000098.
Values sent between devices are 32-bit elements; how exact they have to be, the bound alone decides.
No kernel may reach another device: no remote copies, remote signals or barrier semaphores. Data moves between devices by JAX's collectives and lax.ppermute only.
A program may use at most 64 MiB of HBM per device.

```python
import jax
import jax.numpy as jnp
from jax import lax

R = 64
K = 32
MODE_ONE = 2048
MODE_TWO = 1024


def raised(values, own_key, source, target, shards_of, factor):
    def block_of(dim):
        return (jnp.arange(values.shape[dim]) // (values.shape[dim] // shards_of)).reshape((-1,) + (1,) * (values.ndim - 1 - dim))

    near = jax.random.permutation(own_key, shards_of)[block_of(target)]
    far = (block_of(target) + shards_of // 2) % shards_of
    return jnp.where((block_of(source) == near) | (block_of(source) == far), factor * values, values)


def level_of(own_key, shape, split, low, high):
    level = 1.0
    for dim, blocks in split:
        heights = jax.random.uniform(jax.random.fold_in(jax.random.fold_in(own_key, 6), dim), (blocks,), jnp.float32, low / len(split), high / len(split))
        level = level * jnp.repeat(jnp.exp(heights), shape[dim] // blocks).reshape((-1,) + (1,) * (len(shape) - 1 - dim))
    return level


def noise(rng, shape, width, limit, pieces=(), dtype=jnp.bfloat16):
    values = jax.random.normal(rng, shape, jnp.float32) * width
    if len(pieces) > 0:
        values = level_of(rng, shape, pieces, -0.22, 0.18) * values
    return jnp.clip(values, min=-limit, max=limit).astype(dtype)


def gaussian_with(stream_key, extent, width, most, split, heavy, dtype=jnp.bfloat16):
    result = width * jax.random.normal(stream_key, extent, jnp.float32)
    if split:
        result = result * level_of(stream_key, extent, split, -0.22, 0.18)
    return jnp.clip(raised(result, jax.random.fold_in(stream_key, 3), *heavy), -most, most).astype(dtype)


def setup_inputs(seed: int = 0) -> dict:
    keys = jax.random.split(jax.random.key(seed), 4)
    return {
        "tensor": gaussian_with(keys[0], (MODE_ONE, MODE_TWO, K), 1.0, 6.0, ((0, 4), (1, 8)), (1, 0, 8, 2.0), jnp.float32),
        "factor_two": noise(keys[1], (MODE_TWO, R), MODE_TWO ** -0.5, 0.1875, ((0, 8), (1, 4)), jnp.float32),
        "factor_three": noise(keys[2], (K, R), K ** -0.5, 1.0, (), jnp.float32),
    }


def reference(tensor, factor_two, factor_three):
    khatri = (factor_two[:, None, :] * factor_three[None, :, :]).reshape(MODE_TWO * K, R)
    mttkrp = jnp.dot(tensor.reshape(MODE_ONE, MODE_TWO * K), khatri, precision=lax.Precision.HIGHEST)
    gram_two = jnp.dot(factor_two.T, factor_two, precision=lax.Precision.HIGHEST)
    gram_three = jnp.dot(factor_three.T, factor_three, precision=lax.Precision.HIGHEST)
    normal = gram_two * gram_three
    lower = jnp.linalg.cholesky(normal)
    inner = jax.scipy.linalg.solve_triangular(lower, mttkrp.T, lower=True)
    return jax.scipy.linalg.solve_triangular(lower.T, inner, lower=False).T
```

```python
import functools
import math

import jax
import jax.numpy as jnp
from jax import lax
from jax.experimental import pallas as pl
from jax.experimental.pallas import tpu as pltpu
from jax.sharding import PartitionSpec as P

HIGHEST = lax.Precision.HIGHEST
WHOLE = pl.BlockSpec(memory_space=pltpu.VMEM)


def dot_of(left, right, dims):
    return lax.dot_general(
        left, right, ((dims[:1], dims[1:]), ((), ())), precision=HIGHEST, preferred_element_type=jnp.float32
    )


def pack(values):
    half = values.shape[0] // 2
    return jnp.concatenate([values[:half], values[half:]], axis=1)


def rounds_of(size):
    if size == 4:
        return [(2, 3, 1, 0), (3, 2, 0, 1), (1, 0, 3, 2)]
    return [tuple(place ^ distance for place in range(size)) for distance in range(size - 1, 0, -1)]


def pick(table, place):
    value = table[0]
    for index, entry in enumerate(table):
        value = jnp.where(place == index, entry, value)
    return value


def load(tensor_ref, held_ref, sems, firsts):
    rows = held_ref.shape[0] // len(firsts)
    piece = held_ref.shape[0] // sems.shape[0]
    copies = []
    for place, first in enumerate(firsts):
        for start in range(0, rows, piece):
            copies.append(
                pltpu.make_async_copy(
                    tensor_ref.at[pl.ds(first * rows + start, piece)],
                    held_ref.at[pl.ds(place * rows + start, piece)],
                    sems.at[len(copies)],
                )
            )
    for copy in copies:
        copy.start()
    return copies


def halves(values):
    values = values.reshape(values.shape[0] * values.shape[1], values.shape[2])
    high = values.astype(jnp.bfloat16)
    low = (values - high.astype(jnp.float32)).astype(jnp.bfloat16)
    return jnp.concatenate([high, low], axis=1)


def split_kernel(rounds, chunk, tensor_ref, out_ref, held_ref, sems):
    me = lax.axis_index("gy") >> 1
    copies = load(tensor_ref, held_ref, sems, [pick(table, me) for table in rounds])
    depth = held_ref.shape[1]
    piece = held_ref.shape[0] // len(copies)
    for index, copy in enumerate(copies):
        copy.wait()
        for start in range(index * piece, (index + 1) * piece, chunk):
            out_ref[start * depth : (start + chunk) * depth, :] = halves(held_ref[start : start + chunk])


def gram_kernel(*refs):
    *shares, three_ref, gram_ref, three_gram_ref, weight_ref, two_ref = refs
    me = lax.axis_index("gx")
    share = shares[0].shape[0]
    for distance, ref in enumerate(shares):
        two_ref[pl.ds(pl.multiple_of((me ^ distance) * share, share), share), :] = ref[...]
    two = two_ref[...]
    gram_ref[...] = pack(dot_of(two, two, (1, 1)))
    three = three_ref[...]
    three_gram_ref[...] = pack(dot_of(three, three, (0, 0)))
    two = two.T
    high = two.astype(jnp.bfloat16)
    low = (two - high.astype(jnp.float32)).astype(jnp.bfloat16)
    both = jnp.concatenate([high, low], axis=1)
    weight_ref[...] = jnp.concatenate([both, both], axis=0)


def multiply(count, chunk, take, weight_ref, three_ref, outs, sum_ref):
    depth, rank = three_ref.shape
    rows = sum_ref.shape[0]
    half = rows // 2
    three = three_ref[...]
    three = jnp.concatenate([three, three], axis=1)[None]
    lower_half = lax.broadcasted_iota(jnp.int32, (half, 2 * rank), 1) < rank
    for block in range(count):
        for start in range(0, rows, chunk):
            product = jnp.dot(take(block * rows + start), weight_ref[...], preferred_element_type=jnp.float32)
            sum_ref[start : start + chunk, :] = jnp.sum(product.reshape(chunk, depth, 2 * rank) * three, axis=1)
        total = sum_ref[...]
        total = total + pltpu.roll(total, rank, 1)
        place = block % 2 * half
        outs[block // 2][place : place + half, :] = jnp.where(lower_half, total[:half], total[half:])


def sent_kernel(chunk, split_ref, weight_ref, three_ref, gram_ref, *refs):
    *outs, sum_ref = refs
    depth = three_ref.shape[0]

    def take(start):
        return split_ref[start * depth : (start + chunk) * depth, :]

    multiply(2 * len(outs), chunk, take, weight_ref, three_ref, outs, sum_ref)
    for out_ref in outs:
        out_ref[sum_ref.shape[0] :, :] = gram_ref[...]


def kept_kernel(chunk, tensor_ref, weight_ref, three_ref, gram_ref, out_ref, sum_ref, held_ref, sems):
    copies = load(tensor_ref, held_ref, sems, [lax.axis_index("gy") >> 1])
    piece = held_ref.shape[0] // len(copies)

    def take(start):
        if start % piece == 0:
            copies[start // piece].wait()
        return halves(held_ref[start : start + chunk])

    multiply(2, chunk, take, weight_ref, three_ref, [out_ref], sum_ref)
    out_ref[sum_ref.shape[0] :, :] = gram_ref[...]


def add_kernel(left_ref, right_ref, out_ref):
    out_ref[...] = left_ref[...] + right_ref[...]


def combine_kernel(half, left_ref, right_ref, sent_ref, kept_ref):
    bit = lax.rem(lax.axis_index("gy"), 2)
    for out_ref, place in ((sent_ref, 1 - bit), (kept_ref, bit)):
        rows = pl.ds(pl.multiple_of(place * half, half), half)
        out_ref[:half, :] = left_ref[rows, :] + right_ref[rows, :]
        out_ref[half:, :] = left_ref[2 * half :, :] + right_ref[2 * half :, :]


def solve_kernel(left_ref, right_ref, three_gram_ref, out_ref):
    total = left_ref[...] + right_ref[...]
    half, (place, lanes) = out_ref.shape[0] // 2, three_gram_ref.shape
    gram = total[half:] * three_gram_ref[...]
    order = lanes // 2
    rows = lax.broadcasted_iota(jnp.int32, (order, lanes), 0)
    lane_ids = lax.broadcasted_iota(jnp.int32, (order, lanes), 1)
    joined = jnp.concatenate([pltpu.roll(gram, order, 1), gram], axis=0)
    joined = jnp.where(lane_ids < order, jnp.where(rows == lane_ids, 1.0, 0.0), joined)
    right = jnp.concatenate([total[:half], pltpu.roll(total[:half], order, 1)], axis=0)
    right = jnp.where(lax.broadcasted_iota(jnp.int32, right.shape, 1) < order, right, 0.0)

    tile = (8, lanes)
    bands = [joined[8 * g : 8 * g + 8] for g in range(order // 8)]
    places = lax.broadcasted_iota(jnp.int32, tile, 0)

    def lane(value, index):
        return jnp.broadcast_to(value[:, order + index : order + index + 1], tile)

    for own in range(len(bands)):
        base, later = 8 * own, range(own + 1, len(bands))
        line = [jnp.broadcast_to(bands[own][q : q + 1], tile) for q in range(8)]
        entry = [[lane(line[q], base + p) if p >= q else None for p in range(8)] for q in range(8)]
        column = {h: [lane(bands[h], base + q) for q in range(8)] for h in later}
        band = None
        for q in range(8):
            pivot = entry[q][q]
            inverse = pltpu.reciprocal(pivot, approx=True)
            row = line[q] * lax.rsqrt(pivot)
            band = row if band is None else jnp.where(places == q, row, band)
            factor = [entry[q][p] * inverse if p > q else None for p in range(8)]
            for p in range(q + 1, 8):
                entry[p][p] = entry[p][p] - (entry[q][p] * entry[q][p]) * inverse
                for s in range(p + 1, 8):
                    entry[p][s] = entry[p][s] - factor[p] * entry[q][s]
                line[p] = line[p] - factor[p] * line[q]
            for h in later:
                scale = column[h][q] * inverse
                bands[h] = bands[h] - scale * line[q]
                for p in range(q + 1, 8):
                    column[h][p] = column[h][p] - scale * entry[q][p]
        bands[own] = band
    lower = jnp.concatenate(bands, axis=0)
    solved = dot_of(right, lower, (1, 1))
    out_ref[...] = dot_of(solved, lower, (1, 0))[:, :order]


def call(kernel, out_shape, args, flops, limit, scratch=(), specs=None):
    many = isinstance(out_shape, tuple)
    moved = sum(4 * a.size for a in args) + sum(4 * math.prod(o.shape) for o in (out_shape if many else (out_shape,)))
    return pl.pallas_call(
        kernel,
        out_shape=out_shape,
        in_specs=specs or [WHOLE] * len(args),
        out_specs=(WHOLE,) * len(out_shape) if many else WHOLE,
        scratch_shapes=scratch,
        compiler_params=pltpu.CompilerParams(vmem_limit_bytes=limit * 1024 * 1024),
        cost_estimate=pl.CostEstimate(flops=flops, bytes_accessed=moved, transcendentals=0),
    )(*args)


def body(tensor, factor_two, factor_three):
    groups, blocks = lax.axis_size("gx"), lax.axis_size("gy")
    rows, width, depth = tensor.shape
    rank = factor_three.shape[1]
    owned = rows // blocks
    half = owned // 2
    chunk = min(16, half)
    rounds = rounds_of(blocks // 2)
    f32 = functools.partial(pltpu.VMEM, dtype=jnp.float32)
    packed = f32((rank // 2, 2 * rank))
    pair = f32((owned + rank // 2, 2 * rank))
    single = f32((half + rank // 2, 2 * rank))
    sums = f32((owned, 2 * rank))
    hbm = pl.BlockSpec(memory_space=pltpu.HBM)

    def held(size, pieces):
        return [f32((size * 2 * owned, depth, width)), pltpu.SemaphoreType.DMA((size * pieces,))]

    mine = factor_two.T
    shares = [
        lax.ppermute(mine, "gx", [(i, i ^ distance) for i in range(groups)]) for distance in range(groups - 1, 0, -1)
    ]
    shares = [mine] + shares[::-1]
    tensor = pltpu.with_memory_space_constraint(jnp.transpose(tensor, (0, 2, 1)), pltpu.HBM)
    split = call(
        functools.partial(split_kernel, rounds, chunk),
        pltpu.VMEM((len(rounds) * 2 * owned * depth, 2 * width), jnp.bfloat16),
        (tensor,),
        10**9,
        12,
        held(len(rounds), 4),
        [hbm],
    )
    gram, three_gram, weight = call(
        gram_kernel,
        (packed, packed, pltpu.VMEM((2 * width, 2 * rank), jnp.bfloat16)),
        (*shares, factor_three),
        10**8,
        12,
        [f32((rank, width))],
    )
    sent = call(
        functools.partial(sent_kernel, chunk),
        (pair,) * len(rounds),
        (split, weight, factor_three, gram),
        2 * 10**9,
        12,
        [sums],
    )
    arrived = [
        lax.ppermute(
            value, "gy", [(2 * i + bit, 2 * j + bit) for i, j in enumerate(table) for bit in range(2)]
        )
        for value, table in zip(sent, rounds)
    ]
    total = call(
        functools.partial(kept_kernel, chunk),
        pair,
        (tensor, weight, factor_three, gram),
        2 * 10**9,
        12,
        [sums, *held(1, 4)],
        [hbm, WHOLE, WHOLE, WHOLE],
    )
    for part in arrived[:-1]:
        total = call(add_kernel, pair, (total, part), 10**6, 12)
    sent, kept = call(
        functools.partial(combine_kernel, half), (single, single), (total, arrived[-1]), 10**6, 12
    )
    last = lax.ppermute(sent, "gy", [(i, i ^ 1) for i in range(blocks)])
    return call(
        solve_kernel, jax.ShapeDtypeStruct((owned, rank), jnp.float32), (kept, last, three_gram), 10**8, 12
    )


def solution(mesh):
    in_specs = (P("gx", "gy", None), P("gy", "gx"), P())
    out_specs = P(("gx", "gy"), None)
    return jax.shard_map(body, mesh=mesh, in_specs=in_specs, out_specs=out_specs, check_vma=False)
```

```python
import functools
import math

import jax
import jax.numpy as jnp
from jax import lax
from jax.experimental import pallas as pl
from jax.experimental.pallas import tpu as pltpu
from jax.sharding import PartitionSpec as P

HIGHEST = lax.Precision.HIGHEST
WHOLE = pl.BlockSpec(memory_space=pltpu.VMEM)


def dot_of(left, right, dims):
    return lax.dot_general(
        left, right, ((dims[:1], dims[1:]), ((), ())), precision=HIGHEST, preferred_element_type=jnp.float32
    )


def narrow_dot(left, right, dims):
    return lax.dot_general(left, right, ((dims[:1], dims[1:]), ((), ())), preferred_element_type=jnp.float32)


def parted(values):
    high = values.astype(jnp.bfloat16).astype(jnp.float32)
    return high, values - high


def pack(values):
    half = values.shape[0] // 2
    return jnp.concatenate([values[:half], values[half:]], axis=1)


ROUNDS = [(1, 2, 3, 0), (3, 0, 1, 2), (2, 3, 0, 1)]


def pick(table, place):
    value = table[0]
    for index, entry in enumerate(table):
        value = jnp.where(place == index, entry, value)
    return value


def load(tensor_ref, held_ref, sems, firsts):
    rows = held_ref.shape[0] // len(firsts)
    piece = held_ref.shape[0] // sems.shape[0]
    copies = []
    for place, first in enumerate(firsts):
        for start in range(0, rows, piece):
            copies.append(
                pltpu.make_async_copy(
                    tensor_ref.at[pl.ds(first * rows + start, piece)],
                    held_ref.at[pl.ds(place * rows + start, piece)],
                    sems.at[len(copies)],
                )
            )
    for copy in copies:
        copy.start()
    return copies


def halves(values):
    values = values.reshape(values.shape[0] * values.shape[1], values.shape[2])
    high = values.astype(jnp.bfloat16)
    low = (values - high.astype(jnp.float32)).astype(jnp.bfloat16)
    return jnp.concatenate([high, low], axis=1)


def split_kernel(count, chunk, tensor_ref, out_ref, held_ref, sems):
    me = lax.rem(lax.axis_index("gy"), 4)
    firsts = [4 * place + pick(table, me) for table in ROUNDS for place in range(count)]
    copies = load(tensor_ref, held_ref, sems, firsts)
    depth = held_ref.shape[1]
    piece = held_ref.shape[0] // len(copies)
    for index, copy in enumerate(copies):
        copy.wait()
        for start in range(index * piece, (index + 1) * piece, chunk):
            out_ref[start * depth : (start + chunk) * depth, :] = halves(held_ref[start : start + chunk])


def gram_kernel(*refs):
    *shares, three_ref, gram_ref, three_gram_ref, weight_ref, two_ref = refs
    me = lax.axis_index("gx")
    share = shares[0].shape[0]
    for distance, ref in enumerate(shares):
        two_ref[pl.ds(pl.multiple_of((me ^ distance) * share, share), share), :] = ref[...]
    two = two_ref[...]
    gram_ref[...] = pack(dot_of(two, two, (1, 1)))
    three = three_ref[...]
    three_gram_ref[...] = pack(dot_of(three, three, (0, 0)))
    two = two.T
    high = two.astype(jnp.bfloat16)
    low = (two - high.astype(jnp.float32)).astype(jnp.bfloat16)
    both = jnp.concatenate([high, low], axis=1)
    weight_ref[...] = jnp.concatenate([both, both], axis=0)


def multiply(count, chunk, take, weight_ref, three_ref, outs, sum_ref):
    depth, rank = three_ref.shape
    rows = sum_ref.shape[0]
    half = rows // 2
    three = three_ref[...]
    three = jnp.concatenate([three, three], axis=1)[None]
    lower_half = lax.broadcasted_iota(jnp.int32, (half, 2 * rank), 1) < rank
    for block in range(count * len(outs)):
        for start in range(0, rows, chunk):
            product = jnp.dot(take(block * rows + start), weight_ref[...], preferred_element_type=jnp.float32)
            sum_ref[start : start + chunk, :] = jnp.sum(product.reshape(chunk, depth, 2 * rank) * three, axis=1)
        total = sum_ref[...]
        total = total + pltpu.roll(total, rank, 1)
        place = block % count * half
        outs[block // count][place : place + half, :] = jnp.where(lower_half, total[:half], total[half:])


def sent_kernel(count, chunk, split_ref, weight_ref, three_ref, gram_ref, *refs):
    *outs, sum_ref = refs
    depth = three_ref.shape[0]

    def take(start):
        return split_ref[start * depth : (start + chunk) * depth, :]

    multiply(count, chunk, take, weight_ref, three_ref, outs, sum_ref)
    for out_ref in outs:
        out_ref[count * (sum_ref.shape[0] // 2) :, :] = gram_ref[...]


def kept_kernel(count, chunk, tensor_ref, weight_ref, three_ref, gram_ref, out_ref, sum_ref, held_ref, sems):
    me = lax.rem(lax.axis_index("gy"), 4)
    copies = load(tensor_ref, held_ref, sems, [4 * place + me for place in range(count)])
    piece = held_ref.shape[0] // len(copies)

    def take(start):
        if start % piece == 0:
            copies[start // piece].wait()
        return halves(held_ref[start : start + chunk])

    multiply(count, chunk, take, weight_ref, three_ref, [out_ref], sum_ref)
    out_ref[count * (sum_ref.shape[0] // 2) :, :] = gram_ref[...]


def add_kernel(left_ref, right_ref, out_ref):
    out_ref[...] = left_ref[...] + right_ref[...]


def combine_kernel(half, left_ref, right_ref, *out_refs):
    me, count = lax.axis_index("gy") >> 2, len(out_refs)
    for distance, out_ref in enumerate(out_refs):
        rows = pl.ds(pl.multiple_of((me ^ distance) * half, half), half)
        out_ref[:half, :] = left_ref[rows, :] + right_ref[rows, :]
        out_ref[half:, :] = left_ref[count * half :, :] + right_ref[count * half :, :]


def solve_kernel(*refs):
    *parts, three_gram_ref, out_ref = refs
    total = parts[0][...]
    for part in parts[1:]:
        total = total + part[...]
    half, (place, lanes) = out_ref.shape[0] // 2, three_gram_ref.shape
    gram = total[half:] * three_gram_ref[...]
    order = lanes // 2
    rows = lax.broadcasted_iota(jnp.int32, (order, lanes), 0)
    lane_ids = lax.broadcasted_iota(jnp.int32, (order, lanes), 1)
    joined = jnp.concatenate([pltpu.roll(gram, order, 1), gram], axis=0)
    joined = jnp.where(lane_ids < order, jnp.where(rows == lane_ids, 1.0, 0.0), joined)
    right = jnp.concatenate([total[:half], pltpu.roll(total[:half], order, 1)], axis=0)
    right = jnp.where(lax.broadcasted_iota(jnp.int32, right.shape, 1) < order, right, 0.0)

    tile = (8, lanes)
    bands = [joined[8 * g : 8 * g + 8] for g in range(order // 8)]
    places = lax.broadcasted_iota(jnp.int32, tile, 0)

    def lane(value, index):
        return jnp.broadcast_to(value[:, order + index : order + index + 1], tile)

    for own in range(len(bands)):
        base, later = 8 * own, range(own + 1, len(bands))
        line = [jnp.broadcast_to(bands[own][q : q + 1], tile) for q in range(8)]
        across = [lane(bands[own], base + p) for p in range(8)]
        entry = [[jnp.broadcast_to(across[p][q : q + 1], tile) if p >= q else None for p in range(8)] for q in range(8)]
        column = {h: [lane(bands[h], base + q) for q in range(8)] for h in later}
        band = None
        for q in range(8):
            pivot = entry[q][q]
            inverse = pltpu.reciprocal(pivot, approx=True)
            row = line[q] * lax.rsqrt(pivot)
            band = row if band is None else jnp.where(places == q, row, band)
            factor = [entry[q][p] * inverse if p > q else None for p in range(8)]
            for p in range(q + 1, 8):
                entry[p][p] = entry[p][p] - (entry[q][p] * entry[q][p]) * inverse
                for s in range(p + 1, 8):
                    entry[p][s] = entry[p][s] - factor[p] * entry[q][s]
                line[p] = line[p] - factor[p] * line[q]
            for h in later:
                scale = column[h][q] * inverse
                bands[h] = bands[h] - scale * line[q]
                for p in range(q + 1, 8):
                    column[h][p] = column[h][p] - scale * entry[q][p]
        bands[own] = band
    left = lane_ids < order
    lower = jnp.where(left, jnp.concatenate(bands, axis=0), 0.0)
    lower_high, lower_low = parted(lower)
    right_high, right_low = parted(right)
    doubled = lower_high + pltpu.roll(lower_high, order, 1)
    factors = jnp.concatenate([doubled, lower_low], axis=1).astype(jnp.bfloat16)
    terms = jnp.concatenate([right_high + pltpu.roll(right_low, order, 1), right_high], axis=1).astype(jnp.bfloat16)
    solved = narrow_dot(terms, jnp.concatenate([factors, factors], axis=0), (1, 1))
    solved_high, solved_low = parted(solved)
    inside = lax.broadcasted_iota(jnp.int32, solved.shape, 1) < order
    terms = jnp.concatenate(
        [jnp.where(inside, solved_high, solved_low), jnp.where(inside, solved_high, 0.0)], axis=1
    ).astype(jnp.bfloat16)
    factors = jnp.concatenate([lower_high, lower_high, lower_low, lower_low], axis=0).astype(jnp.bfloat16)
    out_ref[...] = narrow_dot(terms, factors, (1, 0))[:, :order]


def call(kernel, out_shape, args, flops, limit, scratch=(), specs=None):
    many = isinstance(out_shape, tuple)
    moved = sum(4 * a.size for a in args) + sum(4 * math.prod(o.shape) for o in (out_shape if many else (out_shape,)))
    return pl.pallas_call(
        kernel,
        out_shape=out_shape,
        in_specs=specs or [WHOLE] * len(args),
        out_specs=(WHOLE,) * len(out_shape) if many else WHOLE,
        scratch_shapes=scratch,
        compiler_params=pltpu.CompilerParams(vmem_limit_bytes=limit * 1024 * 1024),
        cost_estimate=pl.CostEstimate(flops=flops, bytes_accessed=moved, transcendentals=0),
    )(*args)


def body(tensor, factor_two, factor_three):
    groups, blocks = lax.axis_size("gx"), lax.axis_size("gy")
    rows, width, depth = tensor.shape
    rank = factor_three.shape[1]
    owned = rows // blocks
    half = owned // 2
    chunk = min(16, half)
    count = blocks // 4
    f32 = functools.partial(pltpu.VMEM, dtype=jnp.float32)
    packed = f32((rank // 2, 2 * rank))
    group = f32((count * half + rank // 2, 2 * rank))
    single = f32((half + rank // 2, 2 * rank))
    sums = f32((owned, 2 * rank))
    hbm = pl.BlockSpec(memory_space=pltpu.HBM)

    def held(size):
        return [f32((size * owned, depth, width)), pltpu.SemaphoreType.DMA((2 * size,))]

    mine = factor_two.T
    shares = [
        lax.ppermute(mine, "gx", [(i, i ^ distance) for i in range(groups)]) for distance in range(groups - 1, 0, -1)
    ]
    shares = [mine] + shares[::-1]
    tensor = pltpu.with_memory_space_constraint(jnp.transpose(tensor, (0, 2, 1)), pltpu.HBM)
    split = call(
        functools.partial(split_kernel, count, chunk),
        pltpu.VMEM((3 * count * owned * depth, 2 * width), jnp.bfloat16),
        (tensor,),
        10**9,
        12,
        held(3 * count),
        [hbm],
    )
    gram, three_gram, weight = call(
        gram_kernel,
        (packed, packed, pltpu.VMEM((2 * width, 2 * rank), jnp.bfloat16)),
        (*shares, factor_three),
        10**8,
        12,
        [f32((rank, width))],
    )
    sent = call(
        functools.partial(sent_kernel, count, chunk),
        (group,) * len(ROUNDS),
        (split, weight, factor_three, gram),
        2 * 10**9,
        12,
        [sums],
    )
    arrived = [
        lax.ppermute(value, "gy", [(i, i - i % 4 + table[i % 4]) for i in range(blocks)])
        for value, table in zip(sent, ROUNDS)
    ]
    total = call(
        functools.partial(kept_kernel, count, chunk),
        group,
        (tensor, weight, factor_three, gram),
        2 * 10**9,
        12,
        [sums, *held(count)],
        [hbm, WHOLE, WHOLE, WHOLE],
    )
    for part in arrived[:-1]:
        total = call(add_kernel, group, (total, part), 10**6, 12)
    kept, *sent = call(
        functools.partial(combine_kernel, half), (single,) * count, (total, arrived[-1]), 10**6, 12
    )
    parts = [
        lax.ppermute(value, "gy", [(i, i ^ (4 * distance)) for i in range(blocks)])
        for distance, value in enumerate(sent, 1)
    ]
    return call(
        solve_kernel, jax.ShapeDtypeStruct((owned, rank), jnp.float32), (kept, *parts, three_gram), 10**8, 12
    )


def solution(mesh):
    in_specs = (P("gx", "gy", None), P("gy", "gx"), P())
    out_specs = P(("gx", "gy"), None)
    return jax.shard_map(body, mesh=mesh, in_specs=in_specs, out_specs=out_specs, check_vma=False)
```

```python
import functools
import math

import jax
import jax.numpy as jnp
from jax import lax
from jax.experimental import pallas as pl
from jax.experimental.pallas import tpu as pltpu
from jax.sharding import PartitionSpec as P

HIGHEST = lax.Precision.HIGHEST
WHOLE = pl.BlockSpec(memory_space=pltpu.VMEM)


def dot_of(left, right, dims):
    return lax.dot_general(
        left, right, ((dims[:1], dims[1:]), ((), ())), precision=HIGHEST, preferred_element_type=jnp.float32
    )


def pack(values):
    half = values.shape[0] // 2
    return jnp.concatenate([values[:half], values[half:]], axis=1)


ROUNDS = [(1, 2, 3, 0), (3, 0, 1, 2), (2, 3, 0, 1)]


def pick(table, place):
    value = table[0]
    for index, entry in enumerate(table):
        value = jnp.where(place == index, entry, value)
    return value


def load(tensor_ref, held_ref, sems, firsts):
    rows = held_ref.shape[0] // len(firsts)
    piece = held_ref.shape[0] // sems.shape[0]
    copies = []
    for place, first in enumerate(firsts):
        for start in range(0, rows, piece):
            copies.append(
                pltpu.make_async_copy(
                    tensor_ref.at[pl.ds(first * rows + start, piece)],
                    held_ref.at[pl.ds(place * rows + start, piece)],
                    sems.at[len(copies)],
                )
            )
    for copy in copies:
        copy.start()
    return copies


def halves(values):
    values = values.reshape(values.shape[0] * values.shape[1], values.shape[2])
    high = values.astype(jnp.bfloat16)
    low = (values - high.astype(jnp.float32)).astype(jnp.bfloat16)
    return jnp.concatenate([high, low], axis=1)


def split_kernel(count, chunk, tensor_ref, out_ref, held_ref, sems):
    me = lax.rem(lax.axis_index("gy"), 4)
    firsts = [4 * place + pick(table, me) for table in ROUNDS for place in range(count)]
    copies = load(tensor_ref, held_ref, sems, firsts)
    depth = held_ref.shape[1]
    piece = held_ref.shape[0] // len(copies)
    for index, copy in enumerate(copies):
        copy.wait()
        for start in range(index * piece, (index + 1) * piece, chunk):
            out_ref[start * depth : (start + chunk) * depth, :] = halves(held_ref[start : start + chunk])


def multiply(count, chunk, take, weight_ref, three_ref, outs, sum_ref):
    depth, rank = three_ref.shape
    rows = sum_ref.shape[0]
    half = rows // 2
    three = three_ref[...]
    three = jnp.concatenate([three, three], axis=1)[None]
    lower_half = lax.broadcasted_iota(jnp.int32, (half, 2 * rank), 1) < rank
    for block in range(count * len(outs)):
        for start in range(0, rows, chunk):
            product = jnp.dot(take(block * rows + start), weight_ref[...], preferred_element_type=jnp.float32)
            sum_ref[start : start + chunk, :] = jnp.sum(product.reshape(chunk, depth, 2 * rank) * three, axis=1)
        total = sum_ref[...]
        total = total + pltpu.roll(total, rank, 1)
        place = block % count * half
        outs[block // count][place : place + half, :] = jnp.where(lower_half, total[:half], total[half:])


def sent_kernel(groups, count, chunk, split_ref, three_ref, *refs):
    shares, refs = refs[:groups], refs[groups:]
    *outs, gram_ref, three_gram_ref, weight_ref, two_ref, sum_ref = refs
    me = lax.axis_index("gx")
    depth, share = three_ref.shape[0], shares[0].shape[0]
    for distance, ref in enumerate(shares):
        two_ref[pl.ds(pl.multiple_of((me ^ distance) * share, share), share), :] = ref[...]
    two = two_ref[...]
    turned = two.T
    high = turned.astype(jnp.bfloat16)
    low = (turned - high.astype(jnp.float32)).astype(jnp.bfloat16)
    both = jnp.concatenate([high, low], axis=1)
    weight_ref[...] = jnp.concatenate([both, both], axis=0)

    def take(start):
        return split_ref[start * depth : (start + chunk) * depth, :]

    multiply(count, chunk, take, weight_ref, three_ref, outs, sum_ref)
    three = three_ref[...]
    three_gram_ref[...] = pack(dot_of(three, three, (0, 0)))
    gram = pack(dot_of(two, two, (1, 1)))
    gram_ref[...] = gram
    for out_ref in outs:
        out_ref[count * (sum_ref.shape[0] // 2) :, :] = gram


def kept_kernel(count, chunk, tensor_ref, weight_ref, three_ref, gram_ref, out_ref, sum_ref, held_ref, sems):
    me = lax.rem(lax.axis_index("gy"), 4)
    copies = load(tensor_ref, held_ref, sems, [4 * place + me for place in range(count)])
    piece = held_ref.shape[0] // len(copies)

    def take(start):
        if start % piece == 0:
            copies[start // piece].wait()
        return halves(held_ref[start : start + chunk])

    multiply(count, chunk, take, weight_ref, three_ref, [out_ref], sum_ref)
    out_ref[count * (sum_ref.shape[0] // 2) :, :] = gram_ref[...]


def add_kernel(left_ref, right_ref, out_ref):
    out_ref[...] = left_ref[...] + right_ref[...]


def combine_kernel(half, left_ref, right_ref, *out_refs):
    me, count = lax.axis_index("gy") >> 2, len(out_refs)
    for distance, out_ref in enumerate(out_refs):
        rows = pl.ds(pl.multiple_of((me ^ distance) * half, half), half)
        out_ref[:half, :] = left_ref[rows, :] + right_ref[rows, :]
        out_ref[half:, :] = left_ref[count * half :, :] + right_ref[count * half :, :]


def solve_kernel(*refs):
    *parts, three_gram_ref, out_ref = refs
    total = parts[0][...]
    for part in parts[1:]:
        total = total + part[...]
    half, (place, lanes) = out_ref.shape[0] // 2, three_gram_ref.shape
    gram = total[half:] * three_gram_ref[...]
    order = lanes // 2
    rows = lax.broadcasted_iota(jnp.int32, (order, lanes), 0)
    lane_ids = lax.broadcasted_iota(jnp.int32, (order, lanes), 1)
    joined = jnp.concatenate([pltpu.roll(gram, order, 1), gram], axis=0)
    joined = jnp.where(lane_ids < order, jnp.where(rows == lane_ids, 1.0, 0.0), joined)
    right = jnp.concatenate([total[:half], pltpu.roll(total[:half], order, 1)], axis=0)
    right = jnp.where(lax.broadcasted_iota(jnp.int32, right.shape, 1) < order, right, 0.0)

    tile = (8, lanes)
    bands = [joined[8 * g : 8 * g + 8] for g in range(order // 8)]
    places = lax.broadcasted_iota(jnp.int32, tile, 0)

    def lane(value, index):
        return jnp.broadcast_to(value[:, order + index : order + index + 1], tile)

    size, tiles = 16, 2
    for own in range(order // size):
        base, later = size * own, range(tiles * (own + 1), len(bands))
        line = [jnp.broadcast_to(bands[tiles * own + q // 8][q % 8 : q % 8 + 1], tile) for q in range(size)]
        entry = [[lane(line[q], base + p) if p >= q else None for p in range(size)] for q in range(size)]
        column = {h: [lane(bands[h], base + q) for q in range(size)] for h in later}
        done = [None] * tiles
        for q in range(size):
            pivot = entry[q][q]
            inverse = pltpu.reciprocal(pivot, approx=True)
            row = line[q] * lax.rsqrt(pivot)
            done[q // 8] = row if q % 8 == 0 else jnp.where(places == q % 8, row, done[q // 8])
            factor = [entry[q][p] * inverse if p > q else None for p in range(size)]
            for p in range(q + 1, size):
                entry[p][p] = entry[p][p] - (entry[q][p] * entry[q][p]) * inverse
                for s in range(p + 1, size):
                    entry[p][s] = entry[p][s] - factor[p] * entry[q][s]
                line[p] = line[p] - factor[p] * line[q]
            for h in later:
                scale = column[h][q] * inverse
                bands[h] = bands[h] - scale * line[q]
                for p in range(q + 1, size):
                    column[h][p] = column[h][p] - scale * entry[q][p]
        bands[tiles * own : tiles * (own + 1)] = done
    lower = jnp.concatenate(bands, axis=0)
    solved = dot_of(right, lower, (1, 1))
    out_ref[...] = dot_of(solved, lower, (1, 0))[:, :order]


def call(kernel, out_shape, args, flops, limit, scratch=(), specs=None):
    many = isinstance(out_shape, tuple)
    moved = sum(4 * a.size for a in args) + sum(4 * math.prod(o.shape) for o in (out_shape if many else (out_shape,)))
    return pl.pallas_call(
        kernel,
        out_shape=out_shape,
        in_specs=specs or [WHOLE] * len(args),
        out_specs=(WHOLE,) * len(out_shape) if many else WHOLE,
        scratch_shapes=scratch,
        compiler_params=pltpu.CompilerParams(vmem_limit_bytes=limit * 1024 * 1024),
        cost_estimate=pl.CostEstimate(flops=flops, bytes_accessed=moved, transcendentals=0),
    )(*args)


def body(tensor, factor_two, factor_three):
    groups, blocks = lax.axis_size("gx"), lax.axis_size("gy")
    rows, width, depth = tensor.shape
    rank = factor_three.shape[1]
    owned = rows // blocks
    half = owned // 2
    chunk = min(16, half)
    count = blocks // 4
    f32 = functools.partial(pltpu.VMEM, dtype=jnp.float32)
    packed = f32((rank // 2, 2 * rank))
    group = f32((count * half + rank // 2, 2 * rank))
    single = f32((half + rank // 2, 2 * rank))
    sums = f32((owned, 2 * rank))
    hbm = pl.BlockSpec(memory_space=pltpu.HBM)

    def held(size):
        return [f32((size * owned, depth, width)), pltpu.SemaphoreType.DMA((2 * size,))]

    mine = factor_two.T
    shares = [
        lax.ppermute(mine, "gx", [(i, i ^ distance) for i in range(groups)]) for distance in range(groups - 1, 0, -1)
    ]
    shares = [mine] + shares[::-1]
    tensor = pltpu.with_memory_space_constraint(jnp.transpose(tensor, (0, 2, 1)), pltpu.HBM)
    split = call(
        functools.partial(split_kernel, count, chunk),
        pltpu.VMEM((3 * count * owned * depth, 2 * width), jnp.bfloat16),
        (tensor,),
        10**9,
        12,
        held(3 * count),
        [hbm],
    )
    *sent, gram, three_gram, weight = call(
        functools.partial(sent_kernel, groups, count, chunk),
        (group,) * len(ROUNDS) + (packed, packed, pltpu.VMEM((2 * width, 2 * rank), jnp.bfloat16)),
        (split, factor_three, *shares),
        2 * 10**9,
        12,
        [f32((rank, width)), sums],
    )
    arrived = [
        lax.ppermute(value, "gy", [(i, i - i % 4 + table[i % 4]) for i in range(blocks)])
        for value, table in zip(sent, ROUNDS)
    ]
    total = call(
        functools.partial(kept_kernel, count, chunk),
        group,
        (tensor, weight, factor_three, gram),
        2 * 10**9,
        12,
        [sums, *held(count)],
        [hbm, WHOLE, WHOLE, WHOLE],
    )
    for part in arrived[:-1]:
        total = call(add_kernel, group, (total, part), 10**6, 12)
    kept, *sent = call(
        functools.partial(combine_kernel, half), (single,) * count, (total, arrived[-1]), 10**6, 12
    )
    parts = [
        lax.ppermute(value, "gy", [(i, i ^ (4 * distance)) for i in range(blocks)])
        for distance, value in enumerate(sent, 1)
    ]
    return call(
        solve_kernel, jax.ShapeDtypeStruct((owned, rank), jnp.float32), (kept, *parts, three_gram), 10**8, 12
    )


def solution(mesh):
    in_specs = (P("gx", "gy", None), P("gy", "gx"), P())
    out_specs = P(("gx", "gy"), None)
    return jax.shard_map(body, mesh=mesh, in_specs=in_specs, out_specs=out_specs, check_vma=False)
```

```python
import functools
import math

import jax
import jax.numpy as jnp
from jax import lax
from jax.experimental import pallas as pl
from jax.experimental.pallas import tpu as pltpu
from jax.sharding import PartitionSpec as P

HIGHEST = lax.Precision.HIGHEST
WHOLE = pl.BlockSpec(memory_space=pltpu.VMEM)


def dot_of(left, right, dims):
    return lax.dot_general(
        left, right, ((dims[:1], dims[1:]), ((), ())), precision=HIGHEST, preferred_element_type=jnp.float32
    )


def narrow_dot(left, right, dims):
    return lax.dot_general(left, right, ((dims[:1], dims[1:]), ((), ())), preferred_element_type=jnp.float32)


def parted(values):
    high = values.astype(jnp.bfloat16).astype(jnp.float32)
    return high, values - high


def pack(values):
    half = values.shape[0] // 2
    return jnp.concatenate([values[:half], values[half:]], axis=1)


ROUNDS = [(1, 2, 3, 0), (3, 0, 1, 2), (2, 3, 0, 1)]


def pick(table, place):
    value = table[0]
    for index, entry in enumerate(table):
        value = jnp.where(place == index, entry, value)
    return value


def load(tensor_ref, held_ref, sems, firsts):
    rows = held_ref.shape[0] // len(firsts)
    piece = held_ref.shape[0] // sems.shape[0]
    copies = []
    for place, first in enumerate(firsts):
        for start in range(0, rows, piece):
            copies.append(
                pltpu.make_async_copy(
                    tensor_ref.at[pl.ds(first * rows + start, piece)],
                    held_ref.at[pl.ds(place * rows + start, piece)],
                    sems.at[len(copies)],
                )
            )
    for copy in copies:
        copy.start()
    return copies


def halves(values):
    values = values.reshape(values.shape[0] * values.shape[1], values.shape[2])
    high = values.astype(jnp.bfloat16)
    low = (values - high.astype(jnp.float32)).astype(jnp.bfloat16)
    return jnp.concatenate([high, low], axis=1)


def split_kernel(count, chunk, tensor_ref, out_ref, held_ref, sems):
    me = lax.rem(lax.axis_index("gy"), 4)
    firsts = [4 * place + pick(table, me) for table in ROUNDS for place in range(count)]
    copies = load(tensor_ref, held_ref, sems, firsts)
    depth = held_ref.shape[1]
    piece = held_ref.shape[0] // len(copies)
    for index, copy in enumerate(copies):
        copy.wait()
        for start in range(index * piece, (index + 1) * piece, chunk):
            out_ref[start * depth : (start + chunk) * depth, :] = halves(held_ref[start : start + chunk])


def multiply(count, chunk, take, weight_ref, three_ref, outs, sum_ref):
    depth, rank = three_ref.shape
    rows = sum_ref.shape[0]
    half = rows // 2
    three = three_ref[...]
    three = jnp.concatenate([three, three], axis=1)[None]
    lower_half = lax.broadcasted_iota(jnp.int32, (half, 2 * rank), 1) < rank
    for block in range(count * len(outs)):
        for start in range(0, rows, chunk):
            product = jnp.dot(take(block * rows + start), weight_ref[...], preferred_element_type=jnp.float32)
            sum_ref[start : start + chunk, :] = jnp.sum(product.reshape(chunk, depth, 2 * rank) * three, axis=1)
        total = sum_ref[...]
        total = total + pltpu.roll(total, rank, 1)
        place = block % count * half
        outs[block // count][place : place + half, :] = jnp.where(lower_half, total[:half], total[half:])


def sent_kernel(groups, count, chunk, split_ref, three_ref, *refs):
    shares, refs = refs[:groups], refs[groups:]
    *outs, gram_ref, weight_ref, two_ref, sum_ref = refs
    me = lax.axis_index("gx")
    depth, share = three_ref.shape[0], shares[0].shape[0]
    for distance, ref in enumerate(shares):
        two_ref[pl.ds(pl.multiple_of((me ^ distance) * share, share), share), :] = ref[...]
    two = two_ref[...]
    gram = pack(dot_of(two, two, (1, 1)))
    gram_ref[...] = gram
    for out_ref in outs:
        out_ref[count * (sum_ref.shape[0] // 2) :, :] = gram
    turned = two.T
    high = turned.astype(jnp.bfloat16)
    low = (turned - high.astype(jnp.float32)).astype(jnp.bfloat16)
    both = jnp.concatenate([high, low], axis=1)
    weight_ref[...] = jnp.concatenate([both, both], axis=0)

    def take(start):
        return split_ref[start * depth : (start + chunk) * depth, :]

    multiply(count, chunk, take, weight_ref, three_ref, outs, sum_ref)


def kept_kernel(
    count, chunk, tensor_ref, weight_ref, three_ref, gram_ref, out_ref, three_gram_ref, sum_ref, held_ref, sems
):
    me = lax.rem(lax.axis_index("gy"), 4)
    copies = load(tensor_ref, held_ref, sems, [4 * place + me for place in range(count)])
    piece = held_ref.shape[0] // len(copies)

    def take(start):
        if start % piece == 0:
            copies[start // piece].wait()
        return halves(held_ref[start : start + chunk])

    three = three_ref[...]
    three_gram_ref[...] = pack(dot_of(three, three, (0, 0)))
    multiply(count, chunk, take, weight_ref, three_ref, [out_ref], sum_ref)
    out_ref[count * (sum_ref.shape[0] // 2) :, :] = gram_ref[...]


def add_kernel(left_ref, right_ref, out_ref):
    out_ref[...] = left_ref[...] + right_ref[...]


def combine_kernel(half, left_ref, right_ref, *out_refs):
    me, count = lax.axis_index("gy") >> 2, len(out_refs)
    for distance, out_ref in enumerate(out_refs):
        rows = pl.ds(pl.multiple_of((me ^ distance) * half, half), half)
        out_ref[:half, :] = left_ref[rows, :] + right_ref[rows, :]
        out_ref[half:, :] = left_ref[count * half :, :] + right_ref[count * half :, :]


def solve_kernel(*refs):
    *parts, three_gram_ref, out_ref = refs
    total = parts[0][...]
    for part in parts[1:]:
        total = total + part[...]
    half, (place, lanes) = out_ref.shape[0] // 2, three_gram_ref.shape
    gram = total[half:] * three_gram_ref[...]
    order = lanes // 2
    rows = lax.broadcasted_iota(jnp.int32, (order, lanes), 0)
    lane_ids = lax.broadcasted_iota(jnp.int32, (order, lanes), 1)
    joined = jnp.concatenate([pltpu.roll(gram, order, 1), gram], axis=0)
    joined = jnp.where(lane_ids < order, jnp.where(rows == lane_ids, 1.0, 0.0), joined)
    right = jnp.concatenate([total[:half], pltpu.roll(total[:half], order, 1)], axis=0)
    right = jnp.where(lax.broadcasted_iota(jnp.int32, right.shape, 1) < order, right, 0.0)

    tile = (8, lanes)
    bands = [joined[8 * g : 8 * g + 8] for g in range(order // 8)]
    places = lax.broadcasted_iota(jnp.int32, tile, 0)

    def lane(value, index):
        return jnp.broadcast_to(value[:, order + index : order + index + 1], tile)

    for own in range(len(bands)):
        base, later = 8 * own, range(own + 1, len(bands))
        line = [jnp.broadcast_to(bands[own][q : q + 1], tile) for q in range(8)]
        entry = [[lane(line[q], base + p) if p >= q else None for p in range(8)] for q in range(8)]
        column = {h: [lane(bands[h], base + q) for q in range(8)] for h in later}
        band = None
        for q in range(8):
            pivot = entry[q][q]
            inverse = pltpu.reciprocal(pivot, approx=True)
            row = line[q] * lax.rsqrt(pivot)
            band = row if band is None else jnp.where(places == q, row, band)
            factor = [entry[q][p] * inverse if p > q else None for p in range(8)]
            for p in range(q + 1, 8):
                entry[p][p] = entry[p][p] - (entry[q][p] * entry[q][p]) * inverse
                for s in range(p + 1, 8):
                    entry[p][s] = entry[p][s] - factor[p] * entry[q][s]
                line[p] = line[p] - factor[p] * line[q]
            for h in later:
                scale = column[h][q] * inverse
                bands[h] = bands[h] - scale * line[q]
                for p in range(q + 1, 8):
                    column[h][p] = column[h][p] - scale * entry[q][p]
        bands[own] = band
    left = lane_ids < order
    lower = jnp.where(left, jnp.concatenate(bands, axis=0), 0.0)
    lower_high, lower_low = parted(lower)
    right_high, right_low = parted(right)
    doubled = lower_high + pltpu.roll(lower_high, order, 1)
    factors = jnp.concatenate([doubled, lower_low], axis=1).astype(jnp.bfloat16)
    terms = jnp.concatenate([right_high + pltpu.roll(right_low, order, 1), right_high], axis=1).astype(jnp.bfloat16)
    solved = narrow_dot(terms, jnp.concatenate([factors, factors], axis=0), (1, 1))
    solved_high, solved_low = parted(solved)
    inside = lax.broadcasted_iota(jnp.int32, solved.shape, 1) < order
    terms = jnp.concatenate(
        [jnp.where(inside, solved_high, solved_low), jnp.where(inside, solved_high, 0.0)], axis=1
    ).astype(jnp.bfloat16)
    factors = jnp.concatenate([lower_high, lower_high, lower_low, lower_low], axis=0).astype(jnp.bfloat16)
    out_ref[...] = narrow_dot(terms, factors, (1, 0))[:, :order]


def call(kernel, out_shape, args, flops, limit, scratch=(), specs=None):
    many = isinstance(out_shape, tuple)
    moved = sum(4 * a.size for a in args) + sum(4 * math.prod(o.shape) for o in (out_shape if many else (out_shape,)))
    return pl.pallas_call(
        kernel,
        out_shape=out_shape,
        in_specs=specs or [WHOLE] * len(args),
        out_specs=(WHOLE,) * len(out_shape) if many else WHOLE,
        scratch_shapes=scratch,
        compiler_params=pltpu.CompilerParams(vmem_limit_bytes=limit * 1024 * 1024),
        cost_estimate=pl.CostEstimate(flops=flops, bytes_accessed=moved, transcendentals=0),
    )(*args)


def body(tensor, factor_two, factor_three):
    groups, blocks = lax.axis_size("gx"), lax.axis_size("gy")
    rows, width, depth = tensor.shape
    rank = factor_three.shape[1]
    owned = rows // blocks
    half = owned // 2
    chunk = min(16, half)
    count = blocks // 4
    f32 = functools.partial(pltpu.VMEM, dtype=jnp.float32)
    packed = f32((rank // 2, 2 * rank))
    group = f32((count * half + rank // 2, 2 * rank))
    single = f32((half + rank // 2, 2 * rank))
    sums = f32((owned, 2 * rank))
    hbm = pl.BlockSpec(memory_space=pltpu.HBM)

    def held(size):
        return [f32((size * owned, depth, width)), pltpu.SemaphoreType.DMA((2 * size,))]

    mine = factor_two.T
    shares = [
        lax.ppermute(mine, "gx", [(i, i ^ distance) for i in range(groups)]) for distance in range(groups - 1, 0, -1)
    ]
    shares = [mine] + shares[::-1]
    tensor = pltpu.with_memory_space_constraint(jnp.transpose(tensor, (0, 2, 1)), pltpu.HBM)
    split = call(
        functools.partial(split_kernel, count, chunk),
        pltpu.VMEM((3 * count * owned * depth, 2 * width), jnp.bfloat16),
        (tensor,),
        10**9,
        12,
        held(3 * count),
        [hbm],
    )
    *sent, gram, weight = call(
        functools.partial(sent_kernel, groups, count, chunk),
        (group,) * len(ROUNDS) + (packed, pltpu.VMEM((2 * width, 2 * rank), jnp.bfloat16)),
        (split, factor_three, *shares),
        2 * 10**9,
        12,
        [f32((rank, width)), sums],
    )
    arrived = [
        lax.ppermute(value, "gy", [(i, i - i % 4 + table[i % 4]) for i in range(blocks)])
        for value, table in zip(sent, ROUNDS)
    ]
    total, three_gram = call(
        functools.partial(kept_kernel, count, chunk),
        (group, packed),
        (tensor, weight, factor_three, gram),
        2 * 10**9,
        12,
        [sums, *held(count)],
        [hbm, WHOLE, WHOLE, WHOLE],
    )
    for part in arrived[:-1]:
        total = call(add_kernel, group, (total, part), 10**6, 12)
    kept, *sent = call(
        functools.partial(combine_kernel, half), (single,) * count, (total, arrived[-1]), 10**6, 12
    )
    parts = [
        lax.ppermute(value, "gy", [(i, i ^ (4 * distance)) for i in range(blocks)])
        for distance, value in enumerate(sent, 1)
    ]
    return call(
        solve_kernel, jax.ShapeDtypeStruct((owned, rank), jnp.float32), (kept, *parts, three_gram), 10**8, 12
    )


def solution(mesh):
    in_specs = (P("gx", "gy", None), P("gy", "gx"), P())
    out_specs = P(("gx", "gy"), None)
    return jax.shard_map(body, mesh=mesh, in_specs=in_specs, out_specs=out_specs, check_vma=False)
```

```python
import functools
import math

import jax
import jax.numpy as jnp
from jax import lax
from jax.experimental import pallas as pl
from jax.experimental.pallas import tpu as pltpu
from jax.sharding import PartitionSpec as P

HIGHEST = lax.Precision.HIGHEST
WHOLE = pl.BlockSpec(memory_space=pltpu.VMEM)


def dot_of(left, right, dims):
    return lax.dot_general(
        left, right, ((dims[:1], dims[1:]), ((), ())), precision=HIGHEST, preferred_element_type=jnp.float32
    )


def pack(values):
    half = values.shape[0] // 2
    return jnp.concatenate([values[:half], values[half:]], axis=1)


ROUNDS = [(2, 3, 1, 0), (3, 2, 0, 1), (1, 0, 3, 2)]


def pick(table, place):
    value = table[0]
    for index, entry in enumerate(table):
        value = jnp.where(place == index, entry, value)
    return value


def load(tensor_ref, held_ref, sems, firsts):
    rows = held_ref.shape[0] // len(firsts)
    piece = held_ref.shape[0] // sems.shape[0]
    copies = []
    for place, first in enumerate(firsts):
        for start in range(0, rows, piece):
            copies.append(
                pltpu.make_async_copy(
                    tensor_ref.at[pl.ds(first * rows + start, piece)],
                    held_ref.at[pl.ds(place * rows + start, piece)],
                    sems.at[len(copies)],
                )
            )
    for copy in copies:
        copy.start()
    return copies


def halves(values):
    values = values.reshape(values.shape[0] * values.shape[1], values.shape[2])
    high = values.astype(jnp.bfloat16)
    low = (values - high.astype(jnp.float32)).astype(jnp.bfloat16)
    return jnp.concatenate([high, low], axis=1)


def split_kernel(count, chunk, tensor_ref, out_ref, held_ref, sems):
    me = lax.rem(lax.axis_index("gy"), 4)
    firsts = [4 * place + pick(table, me) for table in ROUNDS for place in range(count)]
    copies = load(tensor_ref, held_ref, sems, firsts)
    depth = held_ref.shape[1]
    piece = held_ref.shape[0] // len(copies)
    for index, copy in enumerate(copies):
        copy.wait()
        for start in range(index * piece, (index + 1) * piece, chunk):
            out_ref[start * depth : (start + chunk) * depth, :] = halves(held_ref[start : start + chunk])


def multiply(count, chunk, take, weight_ref, three_ref, outs, sum_ref):
    depth, rank = three_ref.shape
    rows = sum_ref.shape[0]
    half = rows // 2
    three = three_ref[...]
    three = jnp.concatenate([three, three], axis=1)[None]
    lower_half = lax.broadcasted_iota(jnp.int32, (half, 2 * rank), 1) < rank
    for block in range(count * len(outs)):
        for start in range(0, rows, chunk):
            product = jnp.dot(take(block * rows + start), weight_ref[...], preferred_element_type=jnp.float32)
            sum_ref[start : start + chunk, :] = jnp.sum(product.reshape(chunk, depth, 2 * rank) * three, axis=1)
        total = sum_ref[...]
        total = total + pltpu.roll(total, rank, 1)
        place = block % count * half
        outs[block // count][place : place + half, :] = jnp.where(lower_half, total[:half], total[half:])


def sent_kernel(groups, count, chunk, split_ref, three_ref, *refs):
    shares, refs = refs[:groups], refs[groups:]
    *outs, gram_ref, weight_ref, two_ref, sum_ref = refs
    me = lax.axis_index("gx")
    depth, share = three_ref.shape[0], shares[0].shape[0]
    for distance, ref in enumerate(shares):
        two_ref[pl.ds(pl.multiple_of((me ^ distance) * share, share), share), :] = ref[...]
    two = two_ref[...]
    gram = pack(dot_of(two, two, (1, 1)))
    gram_ref[...] = gram
    for out_ref in outs:
        out_ref[count * (sum_ref.shape[0] // 2) :, :] = gram
    turned = two.T
    high = turned.astype(jnp.bfloat16)
    low = (turned - high.astype(jnp.float32)).astype(jnp.bfloat16)
    both = jnp.concatenate([high, low], axis=1)
    weight_ref[...] = jnp.concatenate([both, both], axis=0)

    def take(start):
        return split_ref[start * depth : (start + chunk) * depth, :]

    multiply(count, chunk, take, weight_ref, three_ref, outs, sum_ref)


def kept_kernel(
    count, chunk, tensor_ref, weight_ref, three_ref, gram_ref, out_ref, three_gram_ref, sum_ref, held_ref, sems
):
    me = lax.rem(lax.axis_index("gy"), 4)
    copies = load(tensor_ref, held_ref, sems, [4 * place + me for place in range(count)])
    piece = held_ref.shape[0] // len(copies)

    def take(start):
        if start % piece == 0:
            copies[start // piece].wait()
        return halves(held_ref[start : start + chunk])

    three = three_ref[...]
    three_gram_ref[...] = pack(dot_of(three, three, (0, 0)))
    multiply(count, chunk, take, weight_ref, three_ref, [out_ref], sum_ref)
    out_ref[count * (sum_ref.shape[0] // 2) :, :] = gram_ref[...]


def add_kernel(left_ref, right_ref, out_ref):
    out_ref[...] = left_ref[...] + right_ref[...]


def combine_kernel(half, left_ref, right_ref, *out_refs):
    me, count = lax.axis_index("gy") >> 2, len(out_refs)
    for distance, out_ref in enumerate(out_refs):
        rows = pl.ds(pl.multiple_of((me ^ distance) * half, half), half)
        out_ref[:half, :] = left_ref[rows, :] + right_ref[rows, :]
        out_ref[half:, :] = left_ref[count * half :, :] + right_ref[count * half :, :]


def solve_kernel(*refs):
    *parts, three_gram_ref, out_ref = refs
    total = parts[0][...]
    for part in parts[1:]:
        total = total + part[...]
    half, (place, lanes) = out_ref.shape[0] // 2, three_gram_ref.shape
    gram = total[half:] * three_gram_ref[...]
    order = lanes // 2
    rows = lax.broadcasted_iota(jnp.int32, (order, lanes), 0)
    lane_ids = lax.broadcasted_iota(jnp.int32, (order, lanes), 1)
    joined = jnp.concatenate([pltpu.roll(gram, order, 1), gram], axis=0)
    joined = jnp.where(lane_ids < order, jnp.where(rows == lane_ids, 1.0, 0.0), joined)
    right = jnp.concatenate([total[:half], pltpu.roll(total[:half], order, 1)], axis=0)
    right = jnp.where(lax.broadcasted_iota(jnp.int32, right.shape, 1) < order, right, 0.0)

    tile = (8, lanes)
    bands = [joined[8 * g : 8 * g + 8] for g in range(order // 8)]
    places = lax.broadcasted_iota(jnp.int32, tile, 0)

    def lane(value, index):
        return jnp.broadcast_to(value[:, order + index : order + index + 1], tile)

    for own in range(len(bands)):
        base, later = 8 * own, range(own + 1, len(bands))
        line = [jnp.broadcast_to(bands[own][q : q + 1], tile) for q in range(8)]
        entry = [[lane(line[q], base + p) if p >= q else None for p in range(8)] for q in range(8)]
        column = {h: [lane(bands[h], base + q) for q in range(8)] for h in later}
        band = None
        for q in range(8):
            pivot = entry[q][q]
            inverse = pltpu.reciprocal(pivot, approx=True)
            row = line[q] * lax.rsqrt(pivot)
            band = row if band is None else jnp.where(places == q, row, band)
            factor = [entry[q][p] * inverse if p > q else None for p in range(8)]
            for p in range(q + 1, 8):
                entry[p][p] = entry[p][p] - (entry[q][p] * entry[q][p]) * inverse
                for s in range(p + 1, 8):
                    entry[p][s] = entry[p][s] - factor[p] * entry[q][s]
                line[p] = line[p] - factor[p] * line[q]
            for h in later:
                scale = column[h][q] * inverse
                bands[h] = bands[h] - scale * line[q]
                for p in range(q + 1, 8):
                    column[h][p] = column[h][p] - scale * entry[q][p]
        bands[own] = band
    lower = jnp.concatenate(bands, axis=0)
    solved = dot_of(right, lower, (1, 1))
    out_ref[...] = dot_of(solved, lower, (1, 0))[:, :order]


def call(kernel, out_shape, args, flops, limit, scratch=(), specs=None):
    many = isinstance(out_shape, tuple)
    moved = sum(4 * a.size for a in args) + sum(4 * math.prod(o.shape) for o in (out_shape if many else (out_shape,)))
    return pl.pallas_call(
        kernel,
        out_shape=out_shape,
        in_specs=specs or [WHOLE] * len(args),
        out_specs=(WHOLE,) * len(out_shape) if many else WHOLE,
        scratch_shapes=scratch,
        compiler_params=pltpu.CompilerParams(vmem_limit_bytes=limit * 1024 * 1024),
        cost_estimate=pl.CostEstimate(flops=flops, bytes_accessed=moved, transcendentals=0),
    )(*args)


def body(tensor, factor_two, factor_three):
    groups, blocks = lax.axis_size("gx"), lax.axis_size("gy")
    rows, width, depth = tensor.shape
    rank = factor_three.shape[1]
    owned = rows // blocks
    half = owned // 2
    chunk = min(16, half)
    count = blocks // 4
    f32 = functools.partial(pltpu.VMEM, dtype=jnp.float32)
    packed = f32((rank // 2, 2 * rank))
    group = f32((count * half + rank // 2, 2 * rank))
    single = f32((half + rank // 2, 2 * rank))
    sums = f32((owned, 2 * rank))
    hbm = pl.BlockSpec(memory_space=pltpu.HBM)

    def held(size):
        return [f32((size * owned, depth, width)), pltpu.SemaphoreType.DMA((2 * size,))]

    mine = factor_two.T
    shares = [
        lax.ppermute(mine, "gx", [(i, i ^ distance) for i in range(groups)]) for distance in range(groups - 1, 0, -1)
    ]
    shares = [mine] + shares[::-1]
    tensor = pltpu.with_memory_space_constraint(jnp.transpose(tensor, (0, 2, 1)), pltpu.HBM)
    split = call(
        functools.partial(split_kernel, count, chunk),
        pltpu.VMEM((3 * count * owned * depth, 2 * width), jnp.bfloat16),
        (tensor,),
        10**9,
        12,
        held(3 * count),
        [hbm],
    )
    *sent, gram, weight = call(
        functools.partial(sent_kernel, groups, count, chunk),
        (group,) * len(ROUNDS) + (packed, pltpu.VMEM((2 * width, 2 * rank), jnp.bfloat16)),
        (split, factor_three, *shares),
        2 * 10**9,
        12,
        [f32((rank, width)), sums],
    )
    arrived = [
        lax.ppermute(value, "gy", [(i, i - i % 4 + table[i % 4]) for i in range(blocks)])
        for value, table in zip(sent, ROUNDS)
    ]
    total, three_gram = call(
        functools.partial(kept_kernel, count, chunk),
        (group, packed),
        (tensor, weight, factor_three, gram),
        2 * 10**9,
        12,
        [sums, *held(count)],
        [hbm, WHOLE, WHOLE, WHOLE],
    )
    for part in arrived[:-1]:
        total = call(add_kernel, group, (total, part), 10**6, 12)
    kept, *sent = call(
        functools.partial(combine_kernel, half), (single,) * count, (total, arrived[-1]), 10**6, 12
    )
    parts = [
        lax.ppermute(value, "gy", [(i, i ^ (4 * distance)) for i in range(blocks)])
        for distance, value in enumerate(sent, 1)
    ]
    return call(
        solve_kernel, jax.ShapeDtypeStruct((owned, rank), jnp.float32), (kept, *parts, three_gram), 10**8, 12
    )


def solution(mesh):
    in_specs = (P("gx", "gy", None), P("gy", "gx"), P())
    out_specs = P(("gx", "gy"), None)
    return jax.shard_map(body, mesh=mesh, in_specs=in_specs, out_specs=out_specs, check_vma=False)
```

```python
import functools
import math

import jax
import jax.numpy as jnp
from jax import lax
from jax.experimental import pallas as pl
from jax.experimental.pallas import tpu as pltpu
from jax.sharding import PartitionSpec as P

HIGHEST = lax.Precision.HIGHEST
WHOLE = pl.BlockSpec(memory_space=pltpu.VMEM)


def dot_of(left, right, dims):
    return lax.dot_general(
        left, right, ((dims[:1], dims[1:]), ((), ())), precision=HIGHEST, preferred_element_type=jnp.float32
    )


def pack(values):
    half = values.shape[0] // 2
    return jnp.concatenate([values[:half], values[half:]], axis=1)


ROUNDS = [(3, 2, 1, 0), (2, 3, 0, 1), (1, 0, 3, 2)]


def pick(table, place):
    value = table[0]
    for index, entry in enumerate(table):
        value = jnp.where(place == index, entry, value)
    return value


def load(tensor_ref, held_ref, sems, firsts):
    rows = held_ref.shape[0] // len(firsts)
    piece = held_ref.shape[0] // sems.shape[0]
    copies = []
    for place, first in enumerate(firsts):
        for start in range(0, rows, piece):
            copies.append(
                pltpu.make_async_copy(
                    tensor_ref.at[pl.ds(first * rows + start, piece)],
                    held_ref.at[pl.ds(place * rows + start, piece)],
                    sems.at[len(copies)],
                )
            )
    for copy in copies:
        copy.start()
    return copies


def halves(values):
    values = values.reshape(values.shape[0] * values.shape[1], values.shape[2])
    high = values.astype(jnp.bfloat16)
    low = (values - high.astype(jnp.float32)).astype(jnp.bfloat16)
    return jnp.concatenate([high, low], axis=1)


def split_kernel(count, chunk, tensor_ref, out_ref, held_ref, sems):
    me = lax.rem(lax.axis_index("gy"), 4)
    firsts = [4 * place + pick(table, me) for table in ROUNDS for place in range(count)]
    copies = load(tensor_ref, held_ref, sems, firsts)
    depth = held_ref.shape[1]
    piece = held_ref.shape[0] // len(copies)
    for index, copy in enumerate(copies):
        copy.wait()
        for start in range(index * piece, (index + 1) * piece, chunk):
            out_ref[start * depth : (start + chunk) * depth, :] = halves(held_ref[start : start + chunk])


def multiply(count, chunk, take, weight_ref, three_ref, outs, sum_ref):
    depth, rank = three_ref.shape
    rows = sum_ref.shape[0]
    half = rows // 2
    three = three_ref[...]
    three = jnp.concatenate([three, three], axis=1)[None]
    lower_half = lax.broadcasted_iota(jnp.int32, (half, 2 * rank), 1) < rank
    for block in range(count * len(outs)):
        for start in range(0, rows, chunk):
            product = jnp.dot(take(block * rows + start), weight_ref[...], preferred_element_type=jnp.float32)
            sum_ref[start : start + chunk, :] = jnp.sum(product.reshape(chunk, depth, 2 * rank) * three, axis=1)
        total = sum_ref[...]
        total = total + pltpu.roll(total, rank, 1)
        place = block % count * half
        outs[block // count][place : place + half, :] = jnp.where(lower_half, total[:half], total[half:])


def sent_kernel(groups, count, chunk, split_ref, three_ref, *refs):
    shares, refs = refs[:groups], refs[groups:]
    *outs, gram_ref, weight_ref, two_ref, sum_ref = refs
    me = lax.axis_index("gx")
    depth, share = three_ref.shape[0], shares[0].shape[0]
    for distance, ref in enumerate(shares):
        two_ref[pl.ds(pl.multiple_of((me ^ distance) * share, share), share), :] = ref[...]
    two = two_ref[...]
    gram = pack(dot_of(two, two, (1, 1)))
    gram_ref[...] = gram
    for out_ref in outs:
        out_ref[count * (sum_ref.shape[0] // 2) :, :] = gram
    turned = two.T
    high = turned.astype(jnp.bfloat16)
    low = (turned - high.astype(jnp.float32)).astype(jnp.bfloat16)
    both = jnp.concatenate([high, low], axis=1)
    weight_ref[...] = jnp.concatenate([both, both], axis=0)

    def take(start):
        return split_ref[start * depth : (start + chunk) * depth, :]

    multiply(count, chunk, take, weight_ref, three_ref, outs, sum_ref)


def kept_kernel(
    count, chunk, tensor_ref, weight_ref, three_ref, gram_ref, out_ref, three_gram_ref, sum_ref, held_ref, sems
):
    me = lax.rem(lax.axis_index("gy"), 4)
    copies = load(tensor_ref, held_ref, sems, [4 * place + me for place in range(count)])
    piece = held_ref.shape[0] // len(copies)

    def take(start):
        if start % piece == 0:
            copies[start // piece].wait()
        return halves(held_ref[start : start + chunk])

    three = three_ref[...]
    three_gram_ref[...] = pack(dot_of(three, three, (0, 0)))
    multiply(count, chunk, take, weight_ref, three_ref, [out_ref], sum_ref)
    out_ref[count * (sum_ref.shape[0] // 2) :, :] = gram_ref[...]


def add_kernel(left_ref, right_ref, out_ref):
    out_ref[...] = left_ref[...] + right_ref[...]


def combine_kernel(half, left_ref, right_ref, *out_refs):
    me, count = lax.axis_index("gy") >> 2, len(out_refs)
    for distance, out_ref in enumerate(out_refs):
        rows = pl.ds(pl.multiple_of((me ^ distance) * half, half), half)
        out_ref[:half, :] = left_ref[rows, :] + right_ref[rows, :]
        out_ref[half:, :] = left_ref[count * half :, :] + right_ref[count * half :, :]


def solve_kernel(*refs):
    *parts, three_gram_ref, out_ref = refs
    total = parts[0][...]
    for part in parts[1:]:
        total = total + part[...]
    half, (place, lanes) = out_ref.shape[0] // 2, three_gram_ref.shape
    gram = total[half:] * three_gram_ref[...]
    order = lanes // 2
    rows = lax.broadcasted_iota(jnp.int32, (order, lanes), 0)
    lane_ids = lax.broadcasted_iota(jnp.int32, (order, lanes), 1)
    joined = jnp.concatenate([pltpu.roll(gram, order, 1), gram], axis=0)
    joined = jnp.where(lane_ids < order, jnp.where(rows == lane_ids, 1.0, 0.0), joined)
    right = jnp.concatenate([total[:half], pltpu.roll(total[:half], order, 1)], axis=0)
    right = jnp.where(lax.broadcasted_iota(jnp.int32, right.shape, 1) < order, right, 0.0)

    tile = (8, lanes)
    bands = [joined[8 * g : 8 * g + 8] for g in range(order // 8)]
    places = lax.broadcasted_iota(jnp.int32, tile, 0)

    def lane(value, index):
        return jnp.broadcast_to(value[:, order + index : order + index + 1], tile)

    for own in range(len(bands)):
        base = 8 * own
        line = [jnp.broadcast_to(bands[own][q : q + 1], tile) for q in range(8)]
        entry = [[lane(line[q], base + p) if p >= q else None for p in range(8)] for q in range(8)]
        inverse, done = [None] * 8, None

        def follow(band, column, q):
            scale = column[q] * inverse[q]
            band = band - scale * line[q]
            for p in range(q + 1, 8):
                column[p] = column[p] - scale * entry[q][p]
            return band

        near = bands[own + 1 : own + 2]
        column = [lane(band, base + q) for band in near for q in range(8)]
        for q in range(8):
            pivot = entry[q][q]
            inverse[q] = pltpu.reciprocal(pivot, approx=True)
            row = line[q] * lax.rsqrt(pivot)
            done = row if done is None else jnp.where(places == q, row, done)
            factor = [entry[q][p] * inverse[q] if p > q else None for p in range(8)]
            for p in range(q + 1, 8):
                entry[p][p] = entry[p][p] - (entry[q][p] * entry[q][p]) * inverse[q]
                for s in range(p + 1, 8):
                    entry[p][s] = entry[p][s] - factor[p] * entry[q][s]
                line[p] = line[p] - factor[p] * line[q]
            if near:
                bands[own + 1] = follow(bands[own + 1], column, q)
        bands[own] = done
        for h in range(own + 2, len(bands)):
            column = [lane(bands[h], base + q) for q in range(8)]
            for q in range(8):
                bands[h] = follow(bands[h], column, q)
    lower = jnp.concatenate(bands, axis=0)
    solved = dot_of(right, lower, (1, 1))
    out_ref[...] = dot_of(solved, lower, (1, 0))[:, :order]


def call(kernel, out_shape, args, flops, limit, scratch=(), specs=None):
    many = isinstance(out_shape, tuple)
    moved = sum(4 * a.size for a in args) + sum(4 * math.prod(o.shape) for o in (out_shape if many else (out_shape,)))
    return pl.pallas_call(
        kernel,
        out_shape=out_shape,
        in_specs=specs or [WHOLE] * len(args),
        out_specs=(WHOLE,) * len(out_shape) if many else WHOLE,
        scratch_shapes=scratch,
        compiler_params=pltpu.CompilerParams(vmem_limit_bytes=limit * 1024 * 1024),
        cost_estimate=pl.CostEstimate(flops=flops, bytes_accessed=moved, transcendentals=0),
    )(*args)


def body(tensor, factor_two, factor_three):
    groups, blocks = lax.axis_size("gx"), lax.axis_size("gy")
    rows, width, depth = tensor.shape
    rank = factor_three.shape[1]
    owned = rows // blocks
    half = owned // 2
    chunk = min(16, half)
    count = blocks // 4
    f32 = functools.partial(pltpu.VMEM, dtype=jnp.float32)
    packed = f32((rank // 2, 2 * rank))
    group = f32((count * half + rank // 2, 2 * rank))
    single = f32((half + rank // 2, 2 * rank))
    sums = f32((owned, 2 * rank))
    hbm = pl.BlockSpec(memory_space=pltpu.HBM)

    def held(size):
        return [f32((size * owned, depth, width)), pltpu.SemaphoreType.DMA((2 * size,))]

    mine = factor_two.T
    shares = [
        lax.ppermute(mine, "gx", [(i, i ^ distance) for i in range(groups)]) for distance in range(groups - 1, 0, -1)
    ]
    shares = [mine] + shares[::-1]
    tensor = pltpu.with_memory_space_constraint(jnp.transpose(tensor, (0, 2, 1)), pltpu.HBM)
    split = call(
        functools.partial(split_kernel, count, chunk),
        pltpu.VMEM((3 * count * owned * depth, 2 * width), jnp.bfloat16),
        (tensor,),
        10**9,
        12,
        held(3 * count),
        [hbm],
    )
    *sent, gram, weight = call(
        functools.partial(sent_kernel, groups, count, chunk),
        (group,) * len(ROUNDS) + (packed, pltpu.VMEM((2 * width, 2 * rank), jnp.bfloat16)),
        (split, factor_three, *shares),
        2 * 10**9,
        12,
        [f32((rank, width)), sums],
    )
    arrived = [
        lax.ppermute(value, "gy", [(i, i - i % 4 + table[i % 4]) for i in range(blocks)])
        for value, table in zip(sent, ROUNDS)
    ]
    total, three_gram = call(
        functools.partial(kept_kernel, count, chunk),
        (group, packed),
        (tensor, weight, factor_three, gram),
        2 * 10**9,
        12,
        [sums, *held(count)],
        [hbm, WHOLE, WHOLE, WHOLE],
    )
    for part in arrived[:-1]:
        total = call(add_kernel, group, (total, part), 10**6, 12)
    kept, *sent = call(
        functools.partial(combine_kernel, half), (single,) * count, (total, arrived[-1]), 10**6, 12
    )
    parts = [
        lax.ppermute(value, "gy", [(i, i ^ (4 * distance)) for i in range(blocks)])
        for distance, value in enumerate(sent, 1)
    ]
    return call(
        solve_kernel, jax.ShapeDtypeStruct((owned, rank), jnp.float32), (kept, *parts, three_gram), 10**8, 12
    )


def solution(mesh):
    in_specs = (P("gx", "gy", None), P("gy", "gx"), P())
    out_specs = P(("gx", "gy"), None)
    return jax.shard_map(body, mesh=mesh, in_specs=in_specs, out_specs=out_specs, check_vma=False)
```

```python
import functools
import math

import jax
import jax.numpy as jnp
from jax import lax
from jax.experimental import pallas as pl
from jax.experimental.pallas import tpu as pltpu
from jax.sharding import PartitionSpec as P

HIGHEST = lax.Precision.HIGHEST
WHOLE = pl.BlockSpec(memory_space=pltpu.VMEM)


def dot_of(left, right, dims):
    return lax.dot_general(
        left, right, ((dims[:1], dims[1:]), ((), ())), precision=HIGHEST, preferred_element_type=jnp.float32
    )


def pack(values):
    half = values.shape[0] // 2
    return jnp.concatenate([values[:half], values[half:]], axis=1)


ROUNDS = [(3, 2, 1, 0), (2, 3, 0, 1), (1, 0, 3, 2)]


def pick(table, place):
    value = table[0]
    for index, entry in enumerate(table):
        value = jnp.where(place == index, entry, value)
    return value


def load(tensor_ref, held_ref, sems, firsts):
    rows = held_ref.shape[0] // len(firsts)
    piece = held_ref.shape[0] // sems.shape[0]
    copies = []
    for place, first in enumerate(firsts):
        for start in range(0, rows, piece):
            copies.append(
                pltpu.make_async_copy(
                    tensor_ref.at[pl.ds(first * rows + start, piece)],
                    held_ref.at[pl.ds(place * rows + start, piece)],
                    sems.at[len(copies)],
                )
            )
    for copy in copies:
        copy.start()
    return copies


def halves(values):
    values = values.reshape(values.shape[0] * values.shape[1], values.shape[2])
    high = values.astype(jnp.bfloat16)
    low = (values - high.astype(jnp.float32)).astype(jnp.bfloat16)
    return jnp.concatenate([high, low], axis=1)


def split_kernel(count, chunk, tensor_ref, out_ref, held_ref, sems):
    me = lax.rem(lax.axis_index("gy"), 4)
    firsts = [4 * place + pick(table, me) for table in ROUNDS for place in range(count)]
    copies = load(tensor_ref, held_ref, sems, firsts)
    depth = held_ref.shape[1]
    piece = held_ref.shape[0] // len(copies)
    for index, copy in enumerate(copies):
        copy.wait()
        for start in range(index * piece, (index + 1) * piece, chunk):
            out_ref[start * depth : (start + chunk) * depth, :] = halves(held_ref[start : start + chunk])


def multiply(count, chunk, take, weight_ref, three_ref, outs, sum_ref):
    depth, rank = three_ref.shape
    rows = sum_ref.shape[0]
    half = rows // 2
    three = three_ref[...]
    three = jnp.concatenate([three, three], axis=1)[None]
    lower_half = lax.broadcasted_iota(jnp.int32, (half, 2 * rank), 1) < rank
    for block in range(count * len(outs)):
        for start in range(0, rows, chunk):
            product = jnp.dot(take(block * rows + start), weight_ref[...], preferred_element_type=jnp.float32)
            sum_ref[start : start + chunk, :] = jnp.sum(product.reshape(chunk, depth, 2 * rank) * three, axis=1)
        total = sum_ref[...]
        total = total + pltpu.roll(total, rank, 1)
        place = block % count * half
        outs[block // count][place : place + half, :] = jnp.where(lower_half, total[:half], total[half:])


def sent_kernel(groups, count, chunk, split_ref, three_ref, *refs):
    shares, refs = refs[:groups], refs[groups:]
    *outs, gram_ref, weight_ref, two_ref, sum_ref = refs
    me = lax.axis_index("gx")
    depth, share = three_ref.shape[0], shares[0].shape[0]
    for distance, ref in enumerate(shares):
        two_ref[pl.ds(pl.multiple_of((me ^ distance) * share, share), share), :] = ref[...]
    two = two_ref[...]
    gram = pack(dot_of(two, two, (1, 1)))
    gram_ref[...] = gram
    for out_ref in outs:
        out_ref[count * (sum_ref.shape[0] // 2) :, :] = gram
    high = two.astype(jnp.bfloat16).astype(jnp.float32)
    both = jnp.concatenate([high, two - high], axis=0).T.astype(jnp.bfloat16)
    weight_ref[...] = jnp.concatenate([both, both], axis=0)

    def take(start):
        return split_ref[start * depth : (start + chunk) * depth, :]

    multiply(count, chunk, take, weight_ref, three_ref, outs, sum_ref)


def kept_kernel(
    count, chunk, tensor_ref, weight_ref, three_ref, gram_ref, out_ref, three_gram_ref, sum_ref, held_ref, sems
):
    me = lax.rem(lax.axis_index("gy"), 4)
    copies = load(tensor_ref, held_ref, sems, [4 * place + me for place in range(count)])
    piece = held_ref.shape[0] // len(copies)

    def take(start):
        if start % piece == 0:
            copies[start // piece].wait()
        return halves(held_ref[start : start + chunk])

    three = three_ref[...]
    three_gram_ref[...] = pack(dot_of(three, three, (0, 0)))
    multiply(count, chunk, take, weight_ref, three_ref, [out_ref], sum_ref)
    out_ref[count * (sum_ref.shape[0] // 2) :, :] = gram_ref[...]


def combine_kernel(half, count, *refs):
    parts, out_refs = refs[:-count], refs[-count:]
    me = lax.axis_index("gy") >> 2

    def total(rows):
        return functools.reduce(jnp.add, [part[rows, :] for part in parts])

    gram = total(slice(count * half, None))
    for distance, out_ref in enumerate(out_refs):
        out_ref[:half, :] = total(pl.ds(pl.multiple_of((me ^ distance) * half, half), half))
        out_ref[half:, :] = gram


def solve_kernel(*refs):
    *parts, three_gram_ref, out_ref, band_ref = refs
    total = parts[0][...]
    for part in parts[1:]:
        total = total + part[...]
    half, (place, lanes) = out_ref.shape[0] // 2, three_gram_ref.shape
    gram = total[half:] * three_gram_ref[...]
    order = lanes // 2
    rows = lax.broadcasted_iota(jnp.int32, (order, lanes), 0)
    lane_ids = lax.broadcasted_iota(jnp.int32, (order, lanes), 1)
    joined = jnp.concatenate([pltpu.roll(gram, order, 1), gram], axis=0)
    joined = jnp.where(lane_ids < order, jnp.where(rows == lane_ids, 1.0, 0.0), joined)
    right = jnp.concatenate([total[:half], pltpu.roll(total[:half], order, 1)], axis=0)
    right = jnp.where(lax.broadcasted_iota(jnp.int32, right.shape, 1) < order, right, 0.0)

    tile = (8, lanes)
    bands = [joined[8 * g : 8 * g + 8] for g in range(order // 8)]
    places = lax.broadcasted_iota(jnp.int32, tile, 0)

    def lane(value, index):
        return jnp.broadcast_to(value[:, order + index : order + index + 1], tile)

    for own in range(len(bands)):
        base = 8 * own
        band_ref[8 * own : 8 * own + 8, :] = bands[own]
        line = [jnp.broadcast_to(band_ref[8 * own + q : 8 * own + q + 1, :], tile) for q in range(8)]
        entry = [[lane(line[q], base + p) if p >= q else None for p in range(8)] for q in range(8)]
        inverse, done = [None] * 8, None

        def follow(band, column, q):
            scale = column[q] * inverse[q]
            band = band - scale * line[q]
            for p in range(q + 1, 8):
                column[p] = column[p] - scale * entry[q][p]
            return band

        near = bands[own + 1 : own + 2]
        column = [lane(band, base + q) for band in near for q in range(8)]
        for q in range(8):
            pivot = entry[q][q]
            inverse[q] = pltpu.reciprocal(pivot, approx=True)
            row = line[q] * lax.rsqrt(pivot)
            done = row if done is None else jnp.where(places == q, row, done)
            factor = [entry[q][p] * inverse[q] if p > q else None for p in range(8)]
            for p in range(q + 1, 8):
                entry[p][p] = entry[p][p] - (entry[q][p] * entry[q][p]) * inverse[q]
                for s in range(p + 1, 8):
                    entry[p][s] = entry[p][s] - factor[p] * entry[q][s]
                line[p] = line[p] - factor[p] * line[q]
            if near:
                bands[own + 1] = follow(bands[own + 1], column, q)
        bands[own] = done
        for h in range(own + 2, len(bands)):
            column = [lane(bands[h], base + q) for q in range(8)]
            for q in range(8):
                bands[h] = follow(bands[h], column, q)
    lower = jnp.concatenate(bands, axis=0)
    solved = dot_of(right, lower, (1, 1))
    out_ref[...] = dot_of(solved, lower, (1, 0))[:, :order]


def call(kernel, out_shape, args, flops, limit, scratch=(), specs=None):
    many = isinstance(out_shape, tuple)
    moved = sum(4 * a.size for a in args) + sum(4 * math.prod(o.shape) for o in (out_shape if many else (out_shape,)))
    return pl.pallas_call(
        kernel,
        out_shape=out_shape,
        in_specs=specs or [WHOLE] * len(args),
        out_specs=(WHOLE,) * len(out_shape) if many else WHOLE,
        scratch_shapes=scratch,
        compiler_params=pltpu.CompilerParams(vmem_limit_bytes=limit * 1024 * 1024),
        cost_estimate=pl.CostEstimate(flops=flops, bytes_accessed=moved, transcendentals=0),
    )(*args)


def body(tensor, factor_two, factor_three):
    groups, blocks = lax.axis_size("gx"), lax.axis_size("gy")
    rows, width, depth = tensor.shape
    rank = factor_three.shape[1]
    owned = rows // blocks
    half = owned // 2
    chunk = min(16, half)
    count = blocks // 4
    f32 = functools.partial(pltpu.VMEM, dtype=jnp.float32)
    packed = f32((rank // 2, 2 * rank))
    group = f32((count * half + rank // 2, 2 * rank))
    single = f32((half + rank // 2, 2 * rank))
    sums = f32((owned, 2 * rank))
    hbm = pl.BlockSpec(memory_space=pltpu.HBM)

    def held(size):
        return [f32((size * owned, depth, width)), pltpu.SemaphoreType.DMA((2 * size,))]

    mine = factor_two.T
    shares = [
        lax.ppermute(mine, "gx", [(i, i ^ distance) for i in range(groups)]) for distance in range(groups - 1, 0, -1)
    ]
    shares = [mine] + shares[::-1]
    tensor = pltpu.with_memory_space_constraint(jnp.transpose(tensor, (0, 2, 1)), pltpu.HBM)
    split = call(
        functools.partial(split_kernel, count, chunk),
        pltpu.VMEM((3 * count * owned * depth, 2 * width), jnp.bfloat16),
        (tensor,),
        10**9,
        12,
        held(3 * count),
        [hbm],
    )
    *sent, gram, weight = call(
        functools.partial(sent_kernel, groups, count, chunk),
        (group,) * len(ROUNDS) + (packed, pltpu.VMEM((2 * width, 2 * rank), jnp.bfloat16)),
        (split, factor_three, *shares),
        2 * 10**9,
        12,
        [f32((rank, width)), sums],
    )
    arrived = [
        lax.ppermute(value, "gy", [(i, i - i % 4 + table[i % 4]) for i in range(blocks)])
        for value, table in zip(sent, ROUNDS)
    ]
    total, three_gram = call(
        functools.partial(kept_kernel, count, chunk),
        (group, packed),
        (tensor, weight, factor_three, gram),
        2 * 10**9,
        12,
        [sums, *held(count)],
        [hbm, WHOLE, WHOLE, WHOLE],
    )
    kept, *sent = call(
        functools.partial(combine_kernel, half, count), (single,) * count, (total, *arrived), 10**6, 12
    )
    parts = [
        lax.ppermute(value, "gy", [(i, i ^ (4 * distance)) for i in range(blocks)])
        for distance, value in enumerate(sent, 1)
    ]
    return call(
        solve_kernel, jax.ShapeDtypeStruct((owned, rank), jnp.float32), (kept, *parts, three_gram), 10**8, 12, [f32((rank, 2 * rank))]
    )


def solution(mesh):
    in_specs = (P("gx", "gy", None), P("gy", "gx"), P())
    out_specs = P(("gx", "gy"), None)
    return jax.shard_map(body, mesh=mesh, in_specs=in_specs, out_specs=out_specs, check_vma=False)
```

```python
import functools
import math

import jax
import jax.numpy as jnp
from jax import lax
from jax.experimental import pallas as pl
from jax.experimental.pallas import tpu as pltpu
from jax.sharding import PartitionSpec as P

HIGHEST = lax.Precision.HIGHEST
WHOLE = pl.BlockSpec(memory_space=pltpu.VMEM)


def dot_of(left, right, dims):
    return lax.dot_general(
        left, right, ((dims[:1], dims[1:]), ((), ())), precision=HIGHEST, preferred_element_type=jnp.float32
    )


def pack(values):
    half = values.shape[0] // 2
    return jnp.concatenate([values[:half], values[half:]], axis=1)


ROUNDS = [(3, 2, 1, 0), (2, 3, 0, 1), (1, 0, 3, 2)]


def pick(table, place):
    value = table[0]
    for index, entry in enumerate(table):
        value = jnp.where(place == index, entry, value)
    return value


def load(tensor_ref, held_ref, sems, firsts):
    rows = held_ref.shape[0] // len(firsts)
    piece = held_ref.shape[0] // sems.shape[0]
    copies = []
    for place, first in enumerate(firsts):
        for start in range(0, rows, piece):
            copies.append(
                pltpu.make_async_copy(
                    tensor_ref.at[pl.ds(first * rows + start, piece)],
                    held_ref.at[pl.ds(place * rows + start, piece)],
                    sems.at[len(copies)],
                )
            )
    for copy in copies:
        copy.start()
    return copies


def halves(values):
    values = values.reshape(values.shape[0] * values.shape[1], values.shape[2])
    high = values.astype(jnp.bfloat16)
    low = (values - high.astype(jnp.float32)).astype(jnp.bfloat16)
    return jnp.concatenate([high, low], axis=1)


def split_kernel(count, chunk, tensor_ref, out_ref, held_ref, sems):
    me = lax.rem(lax.axis_index("gy"), 4)
    firsts = [4 * place + pick(table, me) for table in ROUNDS for place in range(count)]
    copies = load(tensor_ref, held_ref, sems, firsts)
    depth = held_ref.shape[1]
    piece = held_ref.shape[0] // len(copies)
    for index, copy in enumerate(copies):
        copy.wait()
        for start in range(index * piece, (index + 1) * piece, chunk):
            out_ref[start * depth : (start + chunk) * depth, :] = halves(held_ref[start : start + chunk])


def multiply(count, chunk, take, weight_ref, three_ref, outs, sum_ref):
    depth, rank = three_ref.shape
    rows = sum_ref.shape[0]
    half = rows // 2
    three = three_ref[...]
    three = jnp.concatenate([three, three], axis=1)[None]
    lower_half = lax.broadcasted_iota(jnp.int32, (half, 2 * rank), 1) < rank
    for block in range(count * len(outs)):
        for start in range(0, rows, chunk):
            product = jnp.dot(take(block * rows + start), weight_ref[...], preferred_element_type=jnp.float32)
            sum_ref[start : start + chunk, :] = jnp.sum(product.reshape(chunk, depth, 2 * rank) * three, axis=1)
        total = sum_ref[...]
        total = total + pltpu.roll(total, rank, 1)
        place = block % count * half
        outs[block // count][place : place + half, :] = jnp.where(lower_half, total[:half], total[half:])


def sent_kernel(groups, count, chunk, split_ref, three_ref, *refs):
    shares, refs = refs[:groups], refs[groups:]
    *outs, gram_ref, weight_ref, two_ref, sum_ref = refs
    me = lax.axis_index("gx")
    depth, share = three_ref.shape[0], shares[0].shape[0]
    for distance, ref in enumerate(shares):
        two_ref[pl.ds(pl.multiple_of((me ^ distance) * share, share), share), :] = ref[...]
    two = two_ref[...]
    gram = pack(dot_of(two, two, (1, 1)))
    gram_ref[...] = gram
    for out_ref in outs:
        out_ref[count * (sum_ref.shape[0] // 2) :, :] = gram
    high = two.astype(jnp.bfloat16).astype(jnp.float32)
    both = jnp.concatenate([high, two - high], axis=0).T.astype(jnp.bfloat16)
    weight_ref[...] = jnp.concatenate([both, both], axis=0)

    def take(start):
        return split_ref[start * depth : (start + chunk) * depth, :]

    multiply(count, chunk, take, weight_ref, three_ref, outs, sum_ref)


def kept_kernel(
    count, chunk, tensor_ref, weight_ref, three_ref, gram_ref, out_ref, three_gram_ref, sum_ref, held_ref, sems
):
    me = lax.rem(lax.axis_index("gy"), 4)
    copies = load(tensor_ref, held_ref, sems, [4 * place + me for place in range(count)])
    piece = held_ref.shape[0] // len(copies)

    def take(start):
        if start % piece == 0:
            copies[start // piece].wait()
        return halves(held_ref[start : start + chunk])

    three = three_ref[...]
    three_gram_ref[...] = pack(dot_of(three, three, (0, 0)))
    multiply(count, chunk, take, weight_ref, three_ref, [out_ref], sum_ref)
    out_ref[count * (sum_ref.shape[0] // 2) :, :] = gram_ref[...]


def combine_kernel(half, count, *refs):
    parts, out_refs = refs[:-count], refs[-count:]
    me = lax.axis_index("gy") >> 2

    def total(rows):
        return functools.reduce(jnp.add, [part[rows, :] for part in parts])

    gram = total(slice(count * half, None))
    for distance, out_ref in enumerate(out_refs):
        out_ref[:half, :] = total(pl.ds(pl.multiple_of((me ^ distance) * half, half), half))
        out_ref[half:, :] = gram


def solve_kernel(*refs):
    *parts, three_gram_ref, out_ref = refs
    total = parts[0][...]
    for part in parts[1:]:
        total = total + part[...]
    half, (place, lanes) = out_ref.shape[0] // 2, three_gram_ref.shape
    gram = total[half:] * three_gram_ref[...]
    order = lanes // 2
    rows = lax.broadcasted_iota(jnp.int32, (order, lanes), 0)
    lane_ids = lax.broadcasted_iota(jnp.int32, (order, lanes), 1)
    joined = jnp.concatenate([pltpu.roll(gram, order, 1), gram], axis=0)
    diagonal = jnp.where(lane_ids - order == rows, joined, 0.0)
    down = lax.rsqrt(jnp.sum(diagonal, axis=1, keepdims=True))
    over = jnp.sum(diagonal, axis=0, keepdims=True)
    over = lax.rsqrt(jnp.where(lane_ids[:1] < order, 1.0, over))
    joined = down * jnp.where(lane_ids < order, jnp.where(rows == lane_ids, 1.0, 0.0), joined * over)
    right = jnp.concatenate([total[:half], pltpu.roll(total[:half], order, 1)], axis=0)
    right = jnp.where(lax.broadcasted_iota(jnp.int32, right.shape, 1) < order, right, 0.0)

    tile = (8, lanes)
    bands = [joined[8 * g : 8 * g + 8] for g in range(order // 8)]
    places = lax.broadcasted_iota(jnp.int32, tile, 0)

    def lane(value, index):
        return jnp.broadcast_to(value[:, order + index : order + index + 1], tile)

    for own in range(len(bands)):
        base = 8 * own
        line = [jnp.broadcast_to(bands[own][q : q + 1], tile) for q in range(8)]
        entry = [[lane(line[q], base + p) if p >= q else None for p in range(8)] for q in range(8)]
        inverse, done = [None] * 8, None

        def follow(band, column, q):
            scale = column[q] * inverse[q]
            band = band - scale * line[q]
            for p in range(q + 1, 8):
                column[p] = column[p] - scale * entry[q][p]
            return band

        near = bands[own + 1 : own + 2]
        column = [lane(band, base + q) for band in near for q in range(8)]
        for q in range(0, 8, 2):
            r = q + 1
            a, b, c = entry[q][q], entry[q][r], entry[r][r]
            inverse[q] = pltpu.reciprocal(a, approx=True)
            inverse_det = pltpu.reciprocal(a * c - b * b, approx=True)
            inverse[r] = a * inverse_det
            both = inverse[q] * inverse_det
            slope = b * inverse[q]
            line[r] = line[r] - slope * line[q]
            first = line[q] * lax.rsqrt(a)
            second = line[r] * lax.rsqrt(c - b * slope)
            done = first if done is None else jnp.where(places == q, first, done)
            done = jnp.where(places == r, second, done)
            cross = [a * entry[r][p] - b * entry[q][p] if p > r else None for p in range(8)]
            for p in range(r + 1, 8):
                entry[r][p] = cross[p] * inverse[q]
                upper, under = entry[q][p] * inverse[q], cross[p] * inverse_det
                line[p] = line[p] - upper * line[q] - under * line[r]
                under = cross[p] * both
                for s in range(p, 8):
                    if s <= r + 2:
                        fall = (entry[q][p] * entry[q][s]) * inverse[q] + (cross[p] * cross[s]) * both
                    else:
                        fall = upper * entry[q][s] + under * cross[s]
                    entry[p][s] = entry[p][s] - fall
            if near:
                bands[own + 1] = follow(bands[own + 1], column, q)
                bands[own + 1] = follow(bands[own + 1], column, r)
        bands[own] = done
        for h in range(own + 2, len(bands)):
            column = [lane(bands[h], base + q) for q in range(8)]
            for q in range(8):
                bands[h] = follow(bands[h], column, q)
    lower = jnp.concatenate(bands, axis=0)
    solved = dot_of(right, lower, (1, 1))
    out_ref[...] = dot_of(solved, lower, (1, 0))[:, :order]


def call(kernel, out_shape, args, flops, limit, scratch=(), specs=None):
    many = isinstance(out_shape, tuple)
    moved = sum(4 * a.size for a in args) + sum(4 * math.prod(o.shape) for o in (out_shape if many else (out_shape,)))
    return pl.pallas_call(
        kernel,
        out_shape=out_shape,
        in_specs=specs or [WHOLE] * len(args),
        out_specs=(WHOLE,) * len(out_shape) if many else WHOLE,
        scratch_shapes=scratch,
        compiler_params=pltpu.CompilerParams(vmem_limit_bytes=limit * 1024 * 1024),
        cost_estimate=pl.CostEstimate(flops=flops, bytes_accessed=moved, transcendentals=0),
    )(*args)


def body(tensor, factor_two, factor_three):
    groups, blocks = lax.axis_size("gx"), lax.axis_size("gy")
    rows, width, depth = tensor.shape
    rank = factor_three.shape[1]
    owned = rows // blocks
    half = owned // 2
    chunk = min(16, half)
    count = blocks // 4
    f32 = functools.partial(pltpu.VMEM, dtype=jnp.float32)
    packed = f32((rank // 2, 2 * rank))
    group = f32((count * half + rank // 2, 2 * rank))
    single = f32((half + rank // 2, 2 * rank))
    sums = f32((owned, 2 * rank))
    hbm = pl.BlockSpec(memory_space=pltpu.HBM)

    def held(size):
        return [f32((size * owned, depth, width)), pltpu.SemaphoreType.DMA((2 * size,))]

    mine = factor_two.T
    shares = [
        lax.ppermute(mine, "gx", [(i, i ^ distance) for i in range(groups)]) for distance in range(groups - 1, 0, -1)
    ]
    shares = [mine] + shares[::-1]
    tensor = pltpu.with_memory_space_constraint(jnp.transpose(tensor, (0, 2, 1)), pltpu.HBM)
    split = call(
        functools.partial(split_kernel, count, chunk),
        pltpu.VMEM((3 * count * owned * depth, 2 * width), jnp.bfloat16),
        (tensor,),
        10**9,
        12,
        held(3 * count),
        [hbm],
    )
    *sent, gram, weight = call(
        functools.partial(sent_kernel, groups, count, chunk),
        (group,) * len(ROUNDS) + (packed, pltpu.VMEM((2 * width, 2 * rank), jnp.bfloat16)),
        (split, factor_three, *shares),
        2 * 10**9,
        12,
        [f32((rank, width)), sums],
    )
    arrived = [
        lax.ppermute(value, "gy", [(i, i - i % 4 + table[i % 4]) for i in range(blocks)])
        for value, table in zip(sent, ROUNDS)
    ]
    total, three_gram = call(
        functools.partial(kept_kernel, count, chunk),
        (group, packed),
        (tensor, weight, factor_three, gram),
        2 * 10**9,
        12,
        [sums, *held(count)],
        [hbm, WHOLE, WHOLE, WHOLE],
    )
    kept, *sent = call(
        functools.partial(combine_kernel, half, count), (single,) * count, (total, *arrived), 10**6, 12
    )
    parts = [
        lax.ppermute(value, "gy", [(i, i ^ (4 * distance)) for i in range(blocks)])
        for distance, value in enumerate(sent, 1)
    ]
    return call(
        solve_kernel, jax.ShapeDtypeStruct((owned, rank), jnp.float32), (kept, *parts, three_gram), 10**8, 12
    )


def solution(mesh):
    in_specs = (P("gx", "gy", None), P("gy", "gx"), P())
    out_specs = P(("gx", "gy"), None)
    return jax.shard_map(body, mesh=mesh, in_specs=in_specs, out_specs=out_specs, check_vma=False)
```

```python
import functools
import math

import jax
import jax.numpy as jnp
from jax import lax
from jax.experimental import pallas as pl
from jax.experimental.pallas import tpu as pltpu
from jax.sharding import PartitionSpec as P

HIGHEST = lax.Precision.HIGHEST
WHOLE = pl.BlockSpec(memory_space=pltpu.VMEM)


def dot_of(left, right, dims):
    return lax.dot_general(
        left, right, ((dims[:1], dims[1:]), ((), ())), precision=HIGHEST, preferred_element_type=jnp.float32
    )


def pack(values):
    half = values.shape[0] // 2
    return jnp.concatenate([values[:half], values[half:]], axis=1)


ROUNDS = [(3, 2, 1, 0), (2, 3, 0, 1), (1, 0, 3, 2)]


def pick(table, place):
    value = table[0]
    for index, entry in enumerate(table):
        value = jnp.where(place == index, entry, value)
    return value


def load(tensor_ref, held_ref, sems, firsts):
    rows = held_ref.shape[0] // len(firsts)
    piece = held_ref.shape[0] // sems.shape[0]
    copies = []
    for place, first in enumerate(firsts):
        for start in range(0, rows, piece):
            copies.append(
                pltpu.make_async_copy(
                    tensor_ref.at[pl.ds(first * rows + start, piece)],
                    held_ref.at[pl.ds(place * rows + start, piece)],
                    sems.at[len(copies)],
                )
            )
    for copy in copies:
        copy.start()
    return copies


def halves(values):
    values = values.reshape(values.shape[0] * values.shape[1], values.shape[2])
    high = values.astype(jnp.bfloat16)
    low = (values - high.astype(jnp.float32)).astype(jnp.bfloat16)
    return jnp.concatenate([high, low], axis=1)


def split_kernel(count, chunk, tensor_ref, out_ref, held_ref, sems):
    me = lax.rem(lax.axis_index("gy"), 4)
    firsts = [4 * place + pick(table, me) for table in ROUNDS for place in range(count)]
    copies = load(tensor_ref, held_ref, sems, firsts)
    depth = held_ref.shape[1]
    piece = held_ref.shape[0] // len(copies)
    for index, copy in enumerate(copies):
        copy.wait()
        for start in range(index * piece, (index + 1) * piece, chunk):
            out_ref[start * depth : (start + chunk) * depth, :] = halves(held_ref[start : start + chunk])


def multiply(count, chunk, take, weight_ref, three_ref, outs, sum_ref):
    depth, rank = three_ref.shape
    rows = sum_ref.shape[0]
    half = rows // 2
    three = three_ref[...]
    three = jnp.concatenate([three, three], axis=1)[None]
    lower_half = lax.broadcasted_iota(jnp.int32, (half, 2 * rank), 1) < rank
    for block in range(count * len(outs)):
        for start in range(0, rows, chunk):
            product = jnp.dot(take(block * rows + start), weight_ref[...], preferred_element_type=jnp.float32)
            sum_ref[start : start + chunk, :] = jnp.sum(product.reshape(chunk, depth, 2 * rank) * three, axis=1)
        total = sum_ref[...]
        total = total + pltpu.roll(total, rank, 1)
        place = block % count * half
        outs[block // count][place : place + half, :] = jnp.where(lower_half, total[:half], total[half:])


def sent_kernel(groups, count, chunk, split_ref, three_ref, *refs):
    shares, refs = refs[:groups], refs[groups:]
    *outs, gram_ref, weight_ref, two_ref, sum_ref = refs
    me = lax.axis_index("gx")
    depth, share = three_ref.shape[0], shares[0].shape[0]
    for distance, ref in enumerate(shares):
        two_ref[pl.ds(pl.multiple_of((me ^ distance) * share, share), share), :] = ref[...]
    two = two_ref[...]
    gram = pack(dot_of(two, two, (1, 1)))
    gram_ref[...] = gram
    for out_ref in outs:
        out_ref[count * (sum_ref.shape[0] // 2) :, :] = gram
    high = two.astype(jnp.bfloat16).astype(jnp.float32)
    both = jnp.concatenate([high, two - high], axis=0).T.astype(jnp.bfloat16)
    weight_ref[...] = jnp.concatenate([both, both], axis=0)

    def take(start):
        return split_ref[start * depth : (start + chunk) * depth, :]

    multiply(count, chunk, take, weight_ref, three_ref, outs, sum_ref)


def kept_kernel(
    count, chunk, tensor_ref, weight_ref, three_ref, gram_ref, out_ref, three_gram_ref, sum_ref, held_ref, sems
):
    me = lax.rem(lax.axis_index("gy"), 4)
    copies = load(tensor_ref, held_ref, sems, [4 * place + me for place in range(count)])
    piece = held_ref.shape[0] // len(copies)

    def take(start):
        if start % piece == 0:
            copies[start // piece].wait()
        return halves(held_ref[start : start + chunk])

    three = three_ref[...]
    three_gram_ref[...] = pack(dot_of(three, three, (0, 0)))
    multiply(count, chunk, take, weight_ref, three_ref, [out_ref], sum_ref)
    out_ref[count * (sum_ref.shape[0] // 2) :, :] = gram_ref[...]


def combine_kernel(half, count, *refs):
    parts, out_refs = refs[:-count], refs[-count:]
    me = lax.axis_index("gy") >> 2

    def total(rows):
        return functools.reduce(jnp.add, [part[rows, :] for part in parts])

    gram = total(slice(count * half, None))
    for distance, out_ref in enumerate(out_refs):
        out_ref[:half, :] = total(pl.ds(pl.multiple_of((me ^ distance) * half, half), half))
        out_ref[half:, :] = gram


def solve_kernel(*refs):
    *parts, three_gram_ref, out_ref, spread_ref = refs
    total = parts[0][...]
    for part in parts[1:]:
        total = total + part[...]
    half, (place, lanes) = out_ref.shape[0] // 2, three_gram_ref.shape
    gram = total[half:] * three_gram_ref[...]
    order = lanes // 2
    rows = lax.broadcasted_iota(jnp.int32, (order, lanes), 0)
    lane_ids = lax.broadcasted_iota(jnp.int32, (order, lanes), 1)
    joined = jnp.concatenate([pltpu.roll(gram, order, 1), gram], axis=0)
    joined = jnp.where(lane_ids < order, jnp.where(rows == lane_ids, 1.0, 0.0), joined)
    right = jnp.concatenate([total[:half], pltpu.roll(total[:half], order, 1)], axis=0)
    right = jnp.where(lax.broadcasted_iota(jnp.int32, right.shape, 1) < order, right, 0.0)

    tile = (8, lanes)
    bands = [joined[8 * g : 8 * g + 8] for g in range(order // 8)]
    places = lax.broadcasted_iota(jnp.int32, tile, 0)

    def lane(value, index):
        return jnp.broadcast_to(value[:, order + index : order + index + 1], tile)

    for own in range(len(bands)):
        base = 8 * own
        spot = 72 * own
        for p in range(8):
            spread_ref[spot + 8 * p : spot + 8 * p + 8, :] = lane(bands[own], base + p)
        spread_ref[spot + 64 : spot + 72, :] = bands[own]

        def spread(place):
            return jnp.broadcast_to(spread_ref[place : place + 1, :], tile)

        line = [spread(spot + 64 + q) for q in range(8)]
        entry = [[spread(spot + 8 * p + q) if p >= q else None for p in range(8)] for q in range(8)]
        inverse, done = [None] * 8, None

        def follow(band, column, q):
            scale = column[q] * inverse[q]
            band = band - scale * line[q]
            for p in range(q + 1, 8):
                column[p] = column[p] - scale * entry[q][p]
            return band

        near = bands[own + 1 : own + 2]
        column = [lane(band, base + q) for band in near for q in range(8)]
        for q in range(8):
            pivot = entry[q][q]
            inverse[q] = pltpu.reciprocal(pivot, approx=True)
            row = line[q] * lax.rsqrt(pivot)
            done = row if done is None else jnp.where(places == q, row, done)
            factor = [entry[q][p] * inverse[q] if p > q else None for p in range(8)]
            for p in range(q + 1, 8):
                entry[p][p] = entry[p][p] - (entry[q][p] * entry[q][p]) * inverse[q]
                for s in range(p + 1, 8):
                    entry[p][s] = entry[p][s] - factor[p] * entry[q][s]
                line[p] = line[p] - factor[p] * line[q]
            if near:
                bands[own + 1] = follow(bands[own + 1], column, q)
        bands[own] = done
        for h in range(own + 2, len(bands)):
            column = [lane(bands[h], base + q) for q in range(8)]
            for q in range(8):
                bands[h] = follow(bands[h], column, q)
    lower = jnp.concatenate(bands, axis=0)
    solved = dot_of(right, lower, (1, 1))
    out_ref[...] = dot_of(solved, lower, (1, 0))[:, :order]


def call(kernel, out_shape, args, flops, limit, scratch=(), specs=None):
    many = isinstance(out_shape, tuple)
    moved = sum(4 * a.size for a in args) + sum(4 * math.prod(o.shape) for o in (out_shape if many else (out_shape,)))
    return pl.pallas_call(
        kernel,
        out_shape=out_shape,
        in_specs=specs or [WHOLE] * len(args),
        out_specs=(WHOLE,) * len(out_shape) if many else WHOLE,
        scratch_shapes=scratch,
        compiler_params=pltpu.CompilerParams(vmem_limit_bytes=limit * 1024 * 1024),
        cost_estimate=pl.CostEstimate(flops=flops, bytes_accessed=moved, transcendentals=0),
    )(*args)


def body(tensor, factor_two, factor_three):
    groups, blocks = lax.axis_size("gx"), lax.axis_size("gy")
    rows, width, depth = tensor.shape
    rank = factor_three.shape[1]
    owned = rows // blocks
    half = owned // 2
    chunk = min(16, half)
    count = blocks // 4
    f32 = functools.partial(pltpu.VMEM, dtype=jnp.float32)
    packed = f32((rank // 2, 2 * rank))
    group = f32((count * half + rank // 2, 2 * rank))
    single = f32((half + rank // 2, 2 * rank))
    sums = f32((owned, 2 * rank))
    hbm = pl.BlockSpec(memory_space=pltpu.HBM)

    def held(size):
        return [f32((size * owned, depth, width)), pltpu.SemaphoreType.DMA((2 * size,))]

    mine = factor_two.T
    shares = [
        lax.ppermute(mine, "gx", [(i, i ^ distance) for i in range(groups)]) for distance in range(groups - 1, 0, -1)
    ]
    shares = [mine] + shares[::-1]
    tensor = pltpu.with_memory_space_constraint(jnp.transpose(tensor, (0, 2, 1)), pltpu.HBM)
    split = call(
        functools.partial(split_kernel, count, chunk),
        pltpu.VMEM((3 * count * owned * depth, 2 * width), jnp.bfloat16),
        (tensor,),
        10**9,
        12,
        held(3 * count),
        [hbm],
    )
    *sent, gram, weight = call(
        functools.partial(sent_kernel, groups, count, chunk),
        (group,) * len(ROUNDS) + (packed, pltpu.VMEM((2 * width, 2 * rank), jnp.bfloat16)),
        (split, factor_three, *shares),
        2 * 10**9,
        12,
        [f32((rank, width)), sums],
    )
    arrived = [
        lax.ppermute(value, "gy", [(i, i - i % 4 + table[i % 4]) for i in range(blocks)])
        for value, table in zip(sent, ROUNDS)
    ]
    total, three_gram = call(
        functools.partial(kept_kernel, count, chunk),
        (group, packed),
        (tensor, weight, factor_three, gram),
        2 * 10**9,
        12,
        [sums, *held(count)],
        [hbm, WHOLE, WHOLE, WHOLE],
    )
    kept, *sent = call(
        functools.partial(combine_kernel, half, count), (single,) * count, (total, *arrived), 10**6, 12
    )
    parts = [
        lax.ppermute(value, "gy", [(i, i ^ (4 * distance)) for i in range(blocks)])
        for distance, value in enumerate(sent, 1)
    ]
    return call(
        solve_kernel, jax.ShapeDtypeStruct((owned, rank), jnp.float32), (kept, *parts, three_gram), 10**8, 12, [f32((9 * rank, 2 * rank))]
    )


def solution(mesh):
    in_specs = (P("gx", "gy", None), P("gy", "gx"), P())
    out_specs = P(("gx", "gy"), None)
    return jax.shard_map(body, mesh=mesh, in_specs=in_specs, out_specs=out_specs, check_vma=False)
```

```python
import functools
import math

import jax
import jax.numpy as jnp
from jax import lax
from jax.experimental import pallas as pl
from jax.experimental.pallas import tpu as pltpu
from jax.sharding import PartitionSpec as P

HIGHEST = lax.Precision.HIGHEST
WHOLE = pl.BlockSpec(memory_space=pltpu.VMEM)


def dot_of(left, right, dims):
    return lax.dot_general(
        left, right, ((dims[:1], dims[1:]), ((), ())), precision=HIGHEST, preferred_element_type=jnp.float32
    )


def pack(values):
    half = values.shape[0] // 2
    return jnp.concatenate([values[:half], values[half:]], axis=1)


ROUNDS = [(3, 2, 1, 0), (2, 3, 0, 1), (1, 0, 3, 2)]


def pick(table, place):
    value = table[0]
    for index, entry in enumerate(table):
        value = jnp.where(place == index, entry, value)
    return value


def load(tensor_ref, held_ref, sems, firsts):
    rows = held_ref.shape[0] // len(firsts)
    piece = held_ref.shape[0] // sems.shape[0]
    copies = []
    for place, first in enumerate(firsts):
        for start in range(0, rows, piece):
            copies.append(
                pltpu.make_async_copy(
                    tensor_ref.at[pl.ds(first * rows + start, piece)],
                    held_ref.at[pl.ds(place * rows + start, piece)],
                    sems.at[len(copies)],
                )
            )
    for copy in copies:
        copy.start()
    return copies


def halves(values):
    values = values.reshape(values.shape[0] * values.shape[1], values.shape[2])
    high = values.astype(jnp.bfloat16)
    low = (values - high.astype(jnp.float32)).astype(jnp.bfloat16)
    return jnp.concatenate([high, low], axis=1)


def split_kernel(count, chunk, tensor_ref, out_ref, held_ref, sems):
    me = lax.rem(lax.axis_index("gy"), 4)
    firsts = [4 * place + pick(table, me) for table in ROUNDS for place in range(count)]
    copies = load(tensor_ref, held_ref, sems, firsts)
    depth = held_ref.shape[1]
    piece = held_ref.shape[0] // len(copies)
    for index, copy in enumerate(copies):
        copy.wait()
        for start in range(index * piece, (index + 1) * piece, chunk):
            out_ref[start * depth : (start + chunk) * depth, :] = halves(held_ref[start : start + chunk])


def folded(rows):
    places = lax.broadcasted_iota(jnp.int32, rows[0].shape, 0)

    def four(x, y):
        low = places < 4
        return jnp.where(low, x, y) + pltpu.roll(jnp.where(low, y, x), 4, 0)

    def two(x, y):
        return jnp.where(places % 4 >= 2, x + pltpu.roll(x, 2, 0), y + pltpu.roll(y, 6, 0))

    def one(x, y):
        return jnp.where(places % 2 == 1, x + pltpu.roll(x, 1, 0), y + pltpu.roll(y, 7, 0))

    odd = two(four(rows[3], rows[7]), four(rows[1], rows[5]))
    even = two(four(rows[2], rows[6]), four(rows[0], rows[4]))
    return one(odd, even)


def multiply(count, chunk, take, weight_ref, three_ref, outs, sum_ref):
    depth, rank = three_ref.shape
    rows = sum_ref.shape[0]
    half = rows // 2
    three = three_ref[...]
    three = jnp.concatenate([three, three], axis=1).reshape(1, depth // 8, 8, 2 * rank)
    lower_half = lax.broadcasted_iota(jnp.int32, (half, 2 * rank), 1) < rank
    for block in range(count * len(outs)):
        for start in range(0, rows, chunk):
            product = jnp.dot(take(block * rows + start), weight_ref[...], preferred_element_type=jnp.float32)
            partial = jnp.sum(product.reshape(chunk, depth // 8, 8, 2 * rank) * three, axis=1)
            for first in range(0, chunk, 8):
                sum_ref[start + first : start + first + 8, :] = folded([partial[first + row] for row in range(8)])
        total = sum_ref[...]
        total = total + pltpu.roll(total, rank, 1)
        place = block % count * half
        outs[block // count][place : place + half, :] = jnp.where(lower_half, total[:half], total[half:])


def sent_kernel(groups, count, chunk, split_ref, three_ref, *refs):
    shares, refs = refs[:groups], refs[groups:]
    *outs, gram_ref, weight_ref, two_ref, sum_ref = refs
    me = lax.axis_index("gx")
    depth, share = three_ref.shape[0], shares[0].shape[0]
    for distance, ref in enumerate(shares):
        two_ref[pl.ds(pl.multiple_of((me ^ distance) * share, share), share), :] = ref[...]
    two = two_ref[...]
    gram = pack(dot_of(two, two, (1, 1)))
    gram_ref[...] = gram
    for out_ref in outs:
        out_ref[count * (sum_ref.shape[0] // 2) :, :] = gram
    high = two.astype(jnp.bfloat16).astype(jnp.float32)
    both = jnp.concatenate([high, two - high], axis=0).T.astype(jnp.bfloat16)
    weight_ref[...] = jnp.concatenate([both, both], axis=0)

    def take(start):
        return split_ref[start * depth : (start + chunk) * depth, :]

    multiply(count, chunk, take, weight_ref, three_ref, outs, sum_ref)


def kept_kernel(
    count, chunk, tensor_ref, weight_ref, three_ref, gram_ref, out_ref, three_gram_ref, sum_ref, held_ref, sems
):
    me = lax.rem(lax.axis_index("gy"), 4)
    copies = load(tensor_ref, held_ref, sems, [4 * place + me for place in range(count)])
    piece = held_ref.shape[0] // len(copies)

    def take(start):
        if start % piece == 0:
            copies[start // piece].wait()
        return halves(held_ref[start : start + chunk])

    three = three_ref[...]
    three_gram_ref[...] = pack(dot_of(three, three, (0, 0)))
    multiply(count, chunk, take, weight_ref, three_ref, [out_ref], sum_ref)
    out_ref[count * (sum_ref.shape[0] // 2) :, :] = gram_ref[...]


def combine_kernel(half, count, *refs):
    parts, out_refs = refs[:-count], refs[-count:]
    me = lax.axis_index("gy") >> 2

    def total(rows):
        return functools.reduce(jnp.add, [part[rows, :] for part in parts])

    gram = total(slice(count * half, None))
    for distance, out_ref in enumerate(out_refs):
        out_ref[:half, :] = total(pl.ds(pl.multiple_of((me ^ distance) * half, half), half))
        out_ref[half:, :] = gram


def solve_kernel(*refs):
    *parts, three_gram_ref, out_ref, spread_ref = refs
    total = parts[0][...]
    for part in parts[1:]:
        total = total + part[...]
    half, (place, lanes) = out_ref.shape[0] // 2, three_gram_ref.shape
    gram = total[half:] * three_gram_ref[...]
    order = lanes // 2
    rows = lax.broadcasted_iota(jnp.int32, (order, lanes), 0)
    lane_ids = lax.broadcasted_iota(jnp.int32, (order, lanes), 1)
    joined = jnp.concatenate([pltpu.roll(gram, order, 1), gram], axis=0)
    joined = jnp.where(lane_ids < order, jnp.where(rows == lane_ids, 1.0, 0.0), joined)
    right = jnp.concatenate([total[:half], pltpu.roll(total[:half], order, 1)], axis=0)
    right = jnp.where(lax.broadcasted_iota(jnp.int32, right.shape, 1) < order, right, 0.0)

    tile = (8, lanes)
    bands = [joined[8 * g : 8 * g + 8] for g in range(order // 8)]
    places = lax.broadcasted_iota(jnp.int32, tile, 0)

    def lane(value, index):
        return jnp.broadcast_to(value[:, order + index : order + index + 1], tile)

    for own in range(len(bands)):
        base = 8 * own
        spot = 72 * own
        for p in range(8):
            spread_ref[spot + 8 * p : spot + 8 * p + 8, :] = lane(bands[own], base + p)
        spread_ref[spot + 64 : spot + 72, :] = bands[own]

        def spread(place):
            return jnp.broadcast_to(spread_ref[place : place + 1, :], tile)

        line = [spread(spot + 64 + q) for q in range(8)]
        entry = [[spread(spot + 8 * p + q) if p >= q else None for p in range(8)] for q in range(8)]
        inverse, done = [None] * 8, None

        def follow(band, column, q):
            scale = column[q] * inverse[q]
            band = band - scale * line[q]
            for p in range(q + 1, 8):
                column[p] = column[p] - scale * entry[q][p]
            return band

        near = bands[own + 1 : own + 2]
        column = [lane(band, base + q) for band in near for q in range(8)]
        for q in range(8):
            pivot = entry[q][q]
            inverse[q] = pltpu.reciprocal(pivot, approx=True)
            row = line[q] * lax.rsqrt(pivot)
            done = row if done is None else jnp.where(places == q, row, done)
            factor = [entry[q][p] * inverse[q] if p > q else None for p in range(8)]
            for p in range(q + 1, 8):
                entry[p][p] = entry[p][p] - (entry[q][p] * entry[q][p]) * inverse[q]
                for s in range(p + 1, 8):
                    entry[p][s] = entry[p][s] - factor[p] * entry[q][s]
                line[p] = line[p] - factor[p] * line[q]
            if near:
                bands[own + 1] = follow(bands[own + 1], column, q)
        bands[own] = done
        for h in range(own + 2, len(bands)):
            column = [lane(bands[h], base + q) for q in range(8)]
            for q in range(8):
                bands[h] = follow(bands[h], column, q)
    lower = jnp.concatenate(bands, axis=0)
    solved = dot_of(right, lower, (1, 1))
    out_ref[...] = dot_of(solved, lower, (1, 0))[:, :order]


def call(kernel, out_shape, args, flops, limit, scratch=(), specs=None):
    many = isinstance(out_shape, tuple)
    moved = sum(4 * a.size for a in args) + sum(4 * math.prod(o.shape) for o in (out_shape if many else (out_shape,)))
    return pl.pallas_call(
        kernel,
        out_shape=out_shape,
        in_specs=specs or [WHOLE] * len(args),
        out_specs=(WHOLE,) * len(out_shape) if many else WHOLE,
        scratch_shapes=scratch,
        compiler_params=pltpu.CompilerParams(vmem_limit_bytes=limit * 1024 * 1024),
        cost_estimate=pl.CostEstimate(flops=flops, bytes_accessed=moved, transcendentals=0),
    )(*args)


def body(tensor, factor_two, factor_three):
    groups, blocks = lax.axis_size("gx"), lax.axis_size("gy")
    rows, width, depth = tensor.shape
    rank = factor_three.shape[1]
    owned = rows // blocks
    half = owned // 2
    chunk = min(16, half)
    count = blocks // 4
    f32 = functools.partial(pltpu.VMEM, dtype=jnp.float32)
    packed = f32((rank // 2, 2 * rank))
    group = f32((count * half + rank // 2, 2 * rank))
    single = f32((half + rank // 2, 2 * rank))
    sums = f32((owned, 2 * rank))
    hbm = pl.BlockSpec(memory_space=pltpu.HBM)

    def held(size):
        return [f32((size * owned, depth, width)), pltpu.SemaphoreType.DMA((2 * size,))]

    mine = factor_two.T
    shares = [
        lax.ppermute(mine, "gx", [(i, i ^ distance) for i in range(groups)]) for distance in range(groups - 1, 0, -1)
    ]
    shares = [mine] + shares[::-1]
    tensor = pltpu.with_memory_space_constraint(jnp.transpose(tensor, (0, 2, 1)), pltpu.HBM)
    split = call(
        functools.partial(split_kernel, count, chunk),
        pltpu.VMEM((3 * count * owned * depth, 2 * width), jnp.bfloat16),
        (tensor,),
        10**9,
        12,
        held(3 * count),
        [hbm],
    )
    *sent, gram, weight = call(
        functools.partial(sent_kernel, groups, count, chunk),
        (group,) * len(ROUNDS) + (packed, pltpu.VMEM((2 * width, 2 * rank), jnp.bfloat16)),
        (split, factor_three, *shares),
        2 * 10**9,
        12,
        [f32((rank, width)), sums],
    )
    arrived = [
        lax.ppermute(value, "gy", [(i, i - i % 4 + table[i % 4]) for i in range(blocks)])
        for value, table in zip(sent, ROUNDS)
    ]
    total, three_gram = call(
        functools.partial(kept_kernel, count, chunk),
        (group, packed),
        (tensor, weight, factor_three, gram),
        2 * 10**9,
        12,
        [sums, *held(count)],
        [hbm, WHOLE, WHOLE, WHOLE],
    )
    kept, *sent = call(
        functools.partial(combine_kernel, half, count), (single,) * count, (total, *arrived), 10**6, 12
    )
    parts = [
        lax.ppermute(value, "gy", [(i, i ^ (4 * distance)) for i in range(blocks)])
        for distance, value in enumerate(sent, 1)
    ]
    return call(
        solve_kernel, jax.ShapeDtypeStruct((owned, rank), jnp.float32), (kept, *parts, three_gram), 10**8, 12, [f32((9 * rank, 2 * rank))]
    )


def solution(mesh):
    in_specs = (P("gx", "gy", None), P("gy", "gx"), P())
    out_specs = P(("gx", "gy"), None)
    return jax.shard_map(body, mesh=mesh, in_specs=in_specs, out_specs=out_specs, check_vma=False)
```

```python
import functools
import math

import jax
import jax.numpy as jnp
from jax import lax
from jax.experimental import pallas as pl
from jax.experimental.pallas import tpu as pltpu
from jax.sharding import PartitionSpec as P

HIGHEST = lax.Precision.HIGHEST
WHOLE = pl.BlockSpec(memory_space=pltpu.VMEM)


def dot_of(left, right, dims):
    return lax.dot_general(
        left, right, ((dims[:1], dims[1:]), ((), ())), precision=HIGHEST, preferred_element_type=jnp.float32
    )


def pack(values):
    half = values.shape[0] // 2
    return jnp.concatenate([values[:half], values[half:]], axis=1)


ROUNDS = [(3, 2, 1, 0), (2, 3, 0, 1), (1, 0, 3, 2)]


def pick(table, place):
    value = table[0]
    for index, entry in enumerate(table):
        value = jnp.where(place == index, entry, value)
    return value


def load(tensor_ref, held_ref, sems, firsts):
    rows = held_ref.shape[0] // len(firsts)
    piece = held_ref.shape[0] // sems.shape[0]
    copies = []
    for place, first in enumerate(firsts):
        for start in range(0, rows, piece):
            copies.append(
                pltpu.make_async_copy(
                    tensor_ref.at[pl.ds(first * rows + start, piece)],
                    held_ref.at[pl.ds(place * rows + start, piece)],
                    sems.at[len(copies)],
                )
            )
    for copy in copies:
        copy.start()
    return copies


def halves(values):
    values = values.reshape(values.shape[0] * values.shape[1], values.shape[2])
    high = values.astype(jnp.bfloat16)
    low = (values - high.astype(jnp.float32)).astype(jnp.bfloat16)
    return jnp.concatenate([high, low], axis=1)


def split_kernel(count, chunk, tensor_ref, out_ref, held_ref, sems):
    me = lax.rem(lax.axis_index("gy"), 4)
    firsts = [4 * place + pick(table, me) for table in ROUNDS for place in range(count)]
    copies = load(tensor_ref, held_ref, sems, firsts)
    depth = held_ref.shape[1]
    piece = held_ref.shape[0] // len(copies)
    for index, copy in enumerate(copies):
        copy.wait()
        for start in range(index * piece, (index + 1) * piece, chunk):
            out_ref[start * depth : (start + chunk) * depth, :] = halves(held_ref[start : start + chunk])


def multiply(count, chunk, take, weight_ref, three_ref, outs, sum_ref):
    depth, rank = three_ref.shape
    rows = sum_ref.shape[0]
    half = rows // 2
    three = three_ref[...]
    three = jnp.concatenate([three, three], axis=1)[None]
    lower_half = lax.broadcasted_iota(jnp.int32, (half, 2 * rank), 1) < rank
    for block in range(count * len(outs)):
        for start in range(0, rows, chunk):
            product = jnp.dot(take(block * rows + start), weight_ref[...], preferred_element_type=jnp.float32)
            sum_ref[start : start + chunk, :] = jnp.sum(product.reshape(chunk, depth, 2 * rank) * three, axis=1)
        total = sum_ref[...]
        total = total + pltpu.roll(total, rank, 1)
        place = block % count * half
        outs[block // count][place : place + half, :] = jnp.where(lower_half, total[:half], total[half:])


def sent_kernel(groups, count, chunk, split_ref, three_ref, *refs):
    shares, refs = refs[:groups], refs[groups:]
    *outs, gram_ref, weight_ref, two_ref, sum_ref = refs
    me = lax.axis_index("gx")
    depth, share = three_ref.shape[0], shares[0].shape[0]
    for distance, ref in enumerate(shares):
        two_ref[pl.ds(pl.multiple_of((me ^ distance) * share, share), share), :] = ref[...]
    two = two_ref[...]
    gram = pack(dot_of(two, two, (1, 1)))
    gram_ref[...] = gram
    for out_ref in outs:
        out_ref[count * (sum_ref.shape[0] // 2) :, :] = gram
    high = two.astype(jnp.bfloat16).astype(jnp.float32)
    both = jnp.concatenate([high, two - high], axis=0).T.astype(jnp.bfloat16)
    weight_ref[...] = jnp.concatenate([both, both], axis=0)

    def take(start):
        return split_ref[start * depth : (start + chunk) * depth, :]

    multiply(count, chunk, take, weight_ref, three_ref, outs, sum_ref)


def kept_kernel(
    count, chunk, tensor_ref, weight_ref, three_ref, gram_ref, out_ref, three_gram_ref, sum_ref, held_ref, sems
):
    me = lax.rem(lax.axis_index("gy"), 4)
    copies = load(tensor_ref, held_ref, sems, [4 * place + me for place in range(count)])
    piece = held_ref.shape[0] // len(copies)

    def take(start):
        if start % piece == 0:
            copies[start // piece].wait()
        return halves(held_ref[start : start + chunk])

    three = three_ref[...]
    three_gram_ref[...] = pack(dot_of(three, three, (0, 0)))
    multiply(count, chunk, take, weight_ref, three_ref, [out_ref], sum_ref)
    out_ref[count * (sum_ref.shape[0] // 2) :, :] = gram_ref[...]


def combine_kernel(half, count, *refs):
    parts, out_refs = refs[:-count], refs[-count:]
    me = lax.axis_index("gy") >> 2

    def total(rows):
        return functools.reduce(jnp.add, [part[rows, :] for part in parts])

    gram = total(slice(count * half, None))
    for distance, out_ref in enumerate(out_refs):
        out_ref[:half, :] = total(pl.ds(pl.multiple_of((me ^ distance) * half, half), half))
        out_ref[half:, :] = gram


def solve_kernel(*refs):
    *parts, three_gram_ref, out_ref, spread_ref = refs
    total = parts[0][...]
    for part in parts[1:]:
        total = total + part[...]
    half, (place, lanes) = out_ref.shape[0] // 2, three_gram_ref.shape
    gram = total[half:] * three_gram_ref[...]
    order = lanes // 2
    rows = lax.broadcasted_iota(jnp.int32, (order, lanes), 0)
    lane_ids = lax.broadcasted_iota(jnp.int32, (order, lanes), 1)
    joined = jnp.concatenate([pltpu.roll(gram, order, 1), gram], axis=0)
    diagonal = jnp.where(lane_ids - order == rows, joined, 0.0)
    down = lax.rsqrt(jnp.sum(diagonal, axis=1, keepdims=True))
    over = jnp.sum(diagonal, axis=0, keepdims=True)
    over = lax.rsqrt(jnp.where(lane_ids[:1] < order, 1.0, over))
    joined = down * jnp.where(lane_ids < order, jnp.where(rows == lane_ids, 1.0, 0.0), joined * over)
    right = jnp.concatenate([total[:half], pltpu.roll(total[:half], order, 1)], axis=0)
    right = jnp.where(lax.broadcasted_iota(jnp.int32, right.shape, 1) < order, right, 0.0)

    tile = (8, lanes)
    bands = [joined[8 * g : 8 * g + 8] for g in range(order // 8)]
    places = lax.broadcasted_iota(jnp.int32, tile, 0)

    def lane(value, index):
        return jnp.broadcast_to(value[:, order + index : order + index + 1], tile)

    for own in range(len(bands)):
        base = 8 * own
        spot = 72 * own
        for p in range(8):
            spread_ref[spot + 8 * p : spot + 8 * p + 8, :] = lane(bands[own], base + p)
        spread_ref[spot + 64 : spot + 72, :] = bands[own]

        def spread(place):
            return jnp.broadcast_to(spread_ref[place : place + 1, :], tile)

        line = [spread(spot + 64 + q) for q in range(8)]
        entry = [[spread(spot + 8 * p + q) if p >= q else None for p in range(8)] for q in range(8)]
        inverse, done = [None] * 8, None

        def follow(band, column, q):
            scale = column[q] * inverse[q]
            band = band - scale * line[q]
            for p in range(q + 1, 8):
                column[p] = column[p] - scale * entry[q][p]
            return band

        near = bands[own + 1 : own + 2]
        column = [lane(band, base + q) for band in near for q in range(8)]
        for q in range(0, 8, 2):
            r = q + 1
            a, b, c = entry[q][q], entry[q][r], entry[r][r]
            inverse[q] = pltpu.reciprocal(a, approx=True)
            inverse_det = pltpu.reciprocal(a * c - b * b, approx=True)
            inverse[r] = a * inverse_det
            both = inverse[q] * inverse_det
            slope = b * inverse[q]
            line[r] = line[r] - slope * line[q]
            first = line[q] * lax.rsqrt(a)
            second = line[r] * lax.rsqrt(c - b * slope)
            done = first if done is None else jnp.where(places == q, first, done)
            done = jnp.where(places == r, second, done)
            cross = [a * entry[r][p] - b * entry[q][p] if p > r else None for p in range(8)]
            for p in range(r + 1, 8):
                entry[r][p] = cross[p] * inverse[q]
                upper, under = entry[q][p] * inverse[q], cross[p] * inverse_det
                line[p] = line[p] - upper * line[q] - under * line[r]
                under = cross[p] * both
                for s in range(p, 8):
                    if s <= r + 2:
                        fall = (entry[q][p] * entry[q][s]) * inverse[q] + (cross[p] * cross[s]) * both
                    else:
                        fall = upper * entry[q][s] + under * cross[s]
                    entry[p][s] = entry[p][s] - fall
            if near:
                bands[own + 1] = follow(bands[own + 1], column, q)
                bands[own + 1] = follow(bands[own + 1], column, r)
        bands[own] = done
        for h in range(own + 2, len(bands)):
            column = [lane(bands[h], base + q) for q in range(8)]
            for q in range(8):
                bands[h] = follow(bands[h], column, q)
    lower = jnp.concatenate(bands, axis=0)
    solved = dot_of(right, lower, (1, 1))
    out_ref[...] = dot_of(solved, lower, (1, 0))[:, :order]


def call(kernel, out_shape, args, flops, limit, scratch=(), specs=None):
    many = isinstance(out_shape, tuple)
    moved = sum(4 * a.size for a in args) + sum(4 * math.prod(o.shape) for o in (out_shape if many else (out_shape,)))
    return pl.pallas_call(
        kernel,
        out_shape=out_shape,
        in_specs=specs or [WHOLE] * len(args),
        out_specs=(WHOLE,) * len(out_shape) if many else WHOLE,
        scratch_shapes=scratch,
        compiler_params=pltpu.CompilerParams(vmem_limit_bytes=limit * 1024 * 1024),
        cost_estimate=pl.CostEstimate(flops=flops, bytes_accessed=moved, transcendentals=0),
    )(*args)


def body(tensor, factor_two, factor_three):
    groups, blocks = lax.axis_size("gx"), lax.axis_size("gy")
    rows, width, depth = tensor.shape
    rank = factor_three.shape[1]
    owned = rows // blocks
    half = owned // 2
    chunk = min(16, half)
    count = blocks // 4
    f32 = functools.partial(pltpu.VMEM, dtype=jnp.float32)
    packed = f32((rank // 2, 2 * rank))
    group = f32((count * half + rank // 2, 2 * rank))
    single = f32((half + rank // 2, 2 * rank))
    sums = f32((owned, 2 * rank))
    hbm = pl.BlockSpec(memory_space=pltpu.HBM)

    def held(size):
        return [f32((size * owned, depth, width)), pltpu.SemaphoreType.DMA((2 * size,))]

    mine = factor_two.T
    shares = [
        lax.ppermute(mine, "gx", [(i, i ^ distance) for i in range(groups)]) for distance in range(groups - 1, 0, -1)
    ]
    shares = [mine] + shares[::-1]
    tensor = pltpu.with_memory_space_constraint(jnp.transpose(tensor, (0, 2, 1)), pltpu.HBM)
    split = call(
        functools.partial(split_kernel, count, chunk),
        pltpu.VMEM((3 * count * owned * depth, 2 * width), jnp.bfloat16),
        (tensor,),
        10**9,
        12,
        held(3 * count),
        [hbm],
    )
    *sent, gram, weight = call(
        functools.partial(sent_kernel, groups, count, chunk),
        (group,) * len(ROUNDS) + (packed, pltpu.VMEM((2 * width, 2 * rank), jnp.bfloat16)),
        (split, factor_three, *shares),
        2 * 10**9,
        12,
        [f32((rank, width)), sums],
    )
    arrived = [
        lax.ppermute(value, "gy", [(i, i - i % 4 + table[i % 4]) for i in range(blocks)])
        for value, table in zip(sent, ROUNDS)
    ]
    total, three_gram = call(
        functools.partial(kept_kernel, count, chunk),
        (group, packed),
        (tensor, weight, factor_three, gram),
        2 * 10**9,
        12,
        [sums, *held(count)],
        [hbm, WHOLE, WHOLE, WHOLE],
    )
    kept, *sent = call(
        functools.partial(combine_kernel, half, count), (single,) * count, (total, *arrived), 10**6, 12
    )
    parts = [
        lax.ppermute(value, "gy", [(i, i ^ (4 * distance)) for i in range(blocks)])
        for distance, value in enumerate(sent, 1)
    ]
    return call(
        solve_kernel, jax.ShapeDtypeStruct((owned, rank), jnp.float32), (kept, *parts, three_gram), 10**8, 12, [f32((9 * rank, 2 * rank))]
    )


def solution(mesh):
    in_specs = (P("gx", "gy", None), P("gy", "gx"), P())
    out_specs = P(("gx", "gy"), None)
    return jax.shard_map(body, mesh=mesh, in_specs=in_specs, out_specs=out_specs, check_vma=False)
```

```python
import functools
import math

import jax
import jax.numpy as jnp
from jax import lax
from jax.experimental import pallas as pl
from jax.experimental.pallas import tpu as pltpu
from jax.sharding import PartitionSpec as P

HIGHEST = lax.Precision.HIGHEST
WHOLE = pl.BlockSpec(memory_space=pltpu.VMEM)


def dot_of(left, right, dims):
    return lax.dot_general(
        left, right, ((dims[:1], dims[1:]), ((), ())), precision=HIGHEST, preferred_element_type=jnp.float32
    )


def pack(values):
    half = values.shape[0] // 2
    return jnp.concatenate([values[:half], values[half:]], axis=1)


ROUNDS = [(3, 2, 1, 0), (2, 3, 0, 1), (1, 0, 3, 2)]


def pick(table, place):
    value = table[0]
    for index, entry in enumerate(table):
        value = jnp.where(place == index, entry, value)
    return value


def load(tensor_ref, held_ref, sems, firsts):
    rows = held_ref.shape[0] // len(firsts)
    piece = held_ref.shape[0] // sems.shape[0]
    copies = []
    for place, first in enumerate(firsts):
        for start in range(0, rows, piece):
            copies.append(
                pltpu.make_async_copy(
                    tensor_ref.at[pl.ds(first * rows + start, piece)],
                    held_ref.at[pl.ds(place * rows + start, piece)],
                    sems.at[len(copies)],
                )
            )
    for copy in copies:
        copy.start()
    return copies


def halves(values):
    values = values.reshape(values.shape[0] * values.shape[1], values.shape[2])
    high = values.astype(jnp.bfloat16)
    low = (values - high.astype(jnp.float32)).astype(jnp.bfloat16)
    return jnp.concatenate([high, low], axis=1)


def split_kernel(count, chunk, tensor_ref, out_ref, held_ref, sems):
    me = lax.rem(lax.axis_index("gy"), 4)
    firsts = [4 * place + pick(table, me) for table in ROUNDS for place in range(count)]
    copies = load(tensor_ref, held_ref, sems, firsts)
    depth = held_ref.shape[1]
    piece = held_ref.shape[0] // len(copies)
    for index, copy in enumerate(copies):
        copy.wait()
        for start in range(index * piece, (index + 1) * piece, chunk):
            out_ref[start * depth : (start + chunk) * depth, :] = halves(held_ref[start : start + chunk])


def multiply(count, chunk, take, weight_ref, three_ref, outs, sum_ref):
    depth, rank = three_ref.shape
    rows = sum_ref.shape[0]
    half = rows // 2
    three = three_ref[...]
    three = jnp.concatenate([three, three], axis=1)[None]
    lower_half = lax.broadcasted_iota(jnp.int32, (half, 2 * rank), 1) < rank
    for block in range(count * len(outs)):
        for start in range(0, rows, chunk):
            product = jnp.dot(take(block * rows + start), weight_ref[...], preferred_element_type=jnp.float32)
            sum_ref[start : start + chunk, :] = jnp.sum(product.reshape(chunk, depth, 2 * rank) * three, axis=1)
        total = sum_ref[...]
        total = total + pltpu.roll(total, rank, 1)
        place = block % count * half
        outs[block // count][place : place + half, :] = jnp.where(lower_half, total[:half], total[half:])


def sent_kernel(groups, count, chunk, split_ref, three_ref, *refs):
    shares, refs = refs[:groups], refs[groups:]
    *outs, gram_ref, weight_ref, two_ref, sum_ref = refs
    me = lax.axis_index("gx")
    depth, share = three_ref.shape[0], shares[0].shape[0]
    for distance, ref in enumerate(shares):
        two_ref[pl.ds(pl.multiple_of((me ^ distance) * share, share), share), :] = ref[...]
    two = two_ref[...]
    gram = pack(dot_of(two, two, (1, 1)))
    gram_ref[...] = gram
    for out_ref in outs:
        out_ref[count * (sum_ref.shape[0] // 2) :, :] = gram
    high = two.astype(jnp.bfloat16).astype(jnp.float32)
    both = jnp.concatenate([high, two - high], axis=0).T.astype(jnp.bfloat16)
    weight_ref[...] = jnp.concatenate([both, both], axis=0)

    def take(start):
        return split_ref[start * depth : (start + chunk) * depth, :]

    multiply(count, chunk, take, weight_ref, three_ref, outs, sum_ref)


def kept_kernel(
    count, chunk, tensor_ref, weight_ref, three_ref, gram_ref, out_ref, three_gram_ref, sum_ref, held_ref, sems
):
    me = lax.rem(lax.axis_index("gy"), 4)
    copies = load(tensor_ref, held_ref, sems, [4 * place + me for place in range(count)])
    piece = held_ref.shape[0] // len(copies)

    def take(start):
        if start % piece == 0:
            copies[start // piece].wait()
        return halves(held_ref[start : start + chunk])

    three = three_ref[...]
    three_gram_ref[...] = pack(dot_of(three, three, (0, 0)))
    multiply(count, chunk, take, weight_ref, three_ref, [out_ref], sum_ref)
    out_ref[count * (sum_ref.shape[0] // 2) :, :] = gram_ref[...]


def combine_kernel(half, count, *refs):
    parts, out_refs = refs[:-count], refs[-count:]
    me = lax.axis_index("gy") >> 2

    def total(rows):
        return functools.reduce(jnp.add, [part[rows, :] for part in parts])

    gram = total(slice(count * half, None))
    for distance, out_ref in enumerate(out_refs):
        out_ref[:half, :] = total(pl.ds(pl.multiple_of((me ^ distance) * half, half), half))
        out_ref[half:, :] = gram


def solve_kernel(*refs):
    *parts, three_gram_ref, out_ref, spread_ref = refs
    total = parts[0][...]
    for part in parts[1:]:
        total = total + part[...]
    half, (place, lanes) = out_ref.shape[0] // 2, three_gram_ref.shape
    gram = total[half:] * three_gram_ref[...]
    order = lanes // 2
    rows = lax.broadcasted_iota(jnp.int32, (order, lanes), 0)
    lane_ids = lax.broadcasted_iota(jnp.int32, (order, lanes), 1)
    joined = jnp.concatenate([pltpu.roll(gram, order, 1), gram], axis=0)
    joined = jnp.where(lane_ids < order, jnp.where(rows == lane_ids, 1.0, 0.0), joined)
    right = jnp.concatenate([total[:half], pltpu.roll(total[:half], order, 1)], axis=0)
    right = jnp.where(lax.broadcasted_iota(jnp.int32, right.shape, 1) < order, right, 0.0)

    tile = (8, lanes)
    bands = [joined[8 * g : 8 * g + 8] for g in range(order // 8)]
    places = lax.broadcasted_iota(jnp.int32, tile, 0)

    def lane(value, index):
        return jnp.broadcast_to(value[:, order + index : order + index + 1], tile)

    for own in range(len(bands)):
        base = 8 * own
        spot = 72 * own
        for p in range(8):
            spread_ref[spot + 8 * p : spot + 8 * p + 8, :] = lane(bands[own], base + p)
        spread_ref[spot + 64 : spot + 72, :] = bands[own]

        def spread(place):
            return jnp.broadcast_to(spread_ref[place : place + 1, :], tile)

        line = [spread(spot + 64 + q) for q in range(8)]
        entry = [[spread(spot + 8 * p + q) if p >= q else None for p in range(8)] for q in range(8)]
        inverse, done = [None] * 8, None

        def follow(band, column, q):
            scale = column[q] * inverse[q]
            band = band - scale * line[q]
            for p in range(q + 1, 8):
                column[p] = column[p] - scale * entry[q][p]
            return band

        later = range(own + 1, len(bands))
        columns = {h: [lane(bands[h], base + q) for q in range(8)] for h in later}
        for q in range(8):
            pivot = entry[q][q]
            inverse[q] = pltpu.reciprocal(pivot, approx=True)
            row = line[q] * lax.rsqrt(pivot)
            done = row if done is None else jnp.where(places == q, row, done)
            factor = [entry[q][p] * inverse[q] if p > q else None for p in range(8)]
            for p in range(q + 1, 8):
                entry[p][p] = entry[p][p] - (entry[q][p] * entry[q][p]) * inverse[q]
                for s in range(p + 1, 8):
                    entry[p][s] = entry[p][s] - factor[p] * entry[q][s]
                line[p] = line[p] - factor[p] * line[q]
            for h in later:
                bands[h] = follow(bands[h], columns[h], q)
        bands[own] = done
    lower = jnp.concatenate(bands, axis=0)
    solved = dot_of(right, lower, (1, 1))
    out_ref[...] = dot_of(solved, lower, (1, 0))[:, :order]


def call(kernel, out_shape, args, flops, limit, scratch=(), specs=None):
    many = isinstance(out_shape, tuple)
    moved = sum(4 * a.size for a in args) + sum(4 * math.prod(o.shape) for o in (out_shape if many else (out_shape,)))
    return pl.pallas_call(
        kernel,
        out_shape=out_shape,
        in_specs=specs or [WHOLE] * len(args),
        out_specs=(WHOLE,) * len(out_shape) if many else WHOLE,
        scratch_shapes=scratch,
        compiler_params=pltpu.CompilerParams(vmem_limit_bytes=limit * 1024 * 1024),
        cost_estimate=pl.CostEstimate(flops=flops, bytes_accessed=moved, transcendentals=0),
    )(*args)


def body(tensor, factor_two, factor_three):
    groups, blocks = lax.axis_size("gx"), lax.axis_size("gy")
    rows, width, depth = tensor.shape
    rank = factor_three.shape[1]
    owned = rows // blocks
    half = owned // 2
    chunk = min(16, half)
    count = blocks // 4
    f32 = functools.partial(pltpu.VMEM, dtype=jnp.float32)
    packed = f32((rank // 2, 2 * rank))
    group = f32((count * half + rank // 2, 2 * rank))
    single = f32((half + rank // 2, 2 * rank))
    sums = f32((owned, 2 * rank))
    hbm = pl.BlockSpec(memory_space=pltpu.HBM)

    def held(size):
        return [f32((size * owned, depth, width)), pltpu.SemaphoreType.DMA((2 * size,))]

    mine = factor_two.T
    shares = [
        lax.ppermute(mine, "gx", [(i, i ^ distance) for i in range(groups)]) for distance in range(groups - 1, 0, -1)
    ]
    shares = [mine] + shares[::-1]
    tensor = pltpu.with_memory_space_constraint(jnp.transpose(tensor, (0, 2, 1)), pltpu.HBM)
    split = call(
        functools.partial(split_kernel, count, chunk),
        pltpu.VMEM((3 * count * owned * depth, 2 * width), jnp.bfloat16),
        (tensor,),
        10**9,
        12,
        held(3 * count),
        [hbm],
    )
    *sent, gram, weight = call(
        functools.partial(sent_kernel, groups, count, chunk),
        (group,) * len(ROUNDS) + (packed, pltpu.VMEM((2 * width, 2 * rank), jnp.bfloat16)),
        (split, factor_three, *shares),
        2 * 10**9,
        12,
        [f32((rank, width)), sums],
    )
    arrived = [
        lax.ppermute(value, "gy", [(i, i - i % 4 + table[i % 4]) for i in range(blocks)])
        for value, table in zip(sent, ROUNDS)
    ]
    total, three_gram = call(
        functools.partial(kept_kernel, count, chunk),
        (group, packed),
        (tensor, weight, factor_three, gram),
        2 * 10**9,
        12,
        [sums, *held(count)],
        [hbm, WHOLE, WHOLE, WHOLE],
    )
    kept, *sent = call(
        functools.partial(combine_kernel, half, count), (single,) * count, (total, *arrived), 10**6, 12
    )
    parts = [
        lax.ppermute(value, "gy", [(i, i ^ (4 * distance)) for i in range(blocks)])
        for distance, value in enumerate(sent, 1)
    ]
    return call(
        solve_kernel, jax.ShapeDtypeStruct((owned, rank), jnp.float32), (kept, *parts, three_gram), 10**8, 12, [f32((9 * rank, 2 * rank))]
    )


def solution(mesh):
    in_specs = (P("gx", "gy", None), P("gy", "gx"), P())
    out_specs = P(("gx", "gy"), None)
    return jax.shard_map(body, mesh=mesh, in_specs=in_specs, out_specs=out_specs, check_vma=False)
```

```python
import functools
import math

import jax
import jax.numpy as jnp
from jax import lax
from jax.experimental import pallas as pl
from jax.experimental.pallas import tpu as pltpu
from jax.sharding import PartitionSpec as P

HIGHEST = lax.Precision.HIGHEST
WHOLE = pl.BlockSpec(memory_space=pltpu.VMEM)


def dot_of(left, right, dims):
    return lax.dot_general(
        left, right, ((dims[:1], dims[1:]), ((), ())), precision=HIGHEST, preferred_element_type=jnp.float32
    )


def pack(values):
    half = values.shape[0] // 2
    return jnp.concatenate([values[:half], values[half:]], axis=1)


ROUNDS = [(3, 2, 1, 0), (2, 3, 0, 1), (1, 0, 3, 2)]


def pick(table, place):
    value = table[0]
    for index, entry in enumerate(table):
        value = jnp.where(place == index, entry, value)
    return value


def load(tensor_ref, held_ref, sems, firsts):
    rows = held_ref.shape[0] // len(firsts)
    piece = held_ref.shape[0] // sems.shape[0]
    copies = []
    for place, first in enumerate(firsts):
        for start in range(0, rows, piece):
            copies.append(
                pltpu.make_async_copy(
                    tensor_ref.at[pl.ds(first * rows + start, piece)],
                    held_ref.at[pl.ds(place * rows + start, piece)],
                    sems.at[len(copies)],
                )
            )
    for copy in copies:
        copy.start()
    return copies


def halves(values):
    values = values.reshape(values.shape[0] * values.shape[1], values.shape[2])
    high = values.astype(jnp.bfloat16)
    low = (values - high.astype(jnp.float32)).astype(jnp.bfloat16)
    return jnp.concatenate([high, low], axis=1)


def split_kernel(count, chunk, tensor_ref, out_ref, held_ref, sems):
    me = lax.rem(lax.axis_index("gy"), 4)
    firsts = [4 * place + pick(table, me) for table in ROUNDS for place in range(count)]
    copies = load(tensor_ref, held_ref, sems, firsts)
    depth = held_ref.shape[1]
    piece = held_ref.shape[0] // len(copies)
    for index, copy in enumerate(copies):
        copy.wait()
        for start in range(index * piece, (index + 1) * piece, chunk):
            out_ref[start * depth : (start + chunk) * depth, :] = halves(held_ref[start : start + chunk])


def multiply(count, chunk, take, weight_ref, three_ref, outs, sum_ref):
    depth, rank = three_ref.shape
    rows = sum_ref.shape[0]
    half = rows // 2
    three = three_ref[...]
    three = jnp.concatenate([three, three], axis=1)[None]
    lower_half = lax.broadcasted_iota(jnp.int32, (half, 2 * rank), 1) < rank
    for block in range(count * len(outs)):
        for start in range(0, rows, chunk):
            product = jnp.dot(take(block * rows + start), weight_ref[...], preferred_element_type=jnp.float32)
            sum_ref[start : start + chunk, :] = jnp.sum(product.reshape(chunk, depth, 2 * rank) * three, axis=1)
        total = sum_ref[...]
        total = total + pltpu.roll(total, rank, 1)
        place = block % count * half
        outs[block // count][place : place + half, :] = jnp.where(lower_half, total[:half], total[half:])


def sent_kernel(groups, count, chunk, split_ref, three_ref, *refs):
    shares, refs = refs[:groups], refs[groups:]
    *outs, gram_ref, weight_ref, two_ref, sum_ref = refs
    me = lax.axis_index("gx")
    depth, share = three_ref.shape[0], shares[0].shape[0]
    for distance, ref in enumerate(shares):
        two_ref[pl.ds(pl.multiple_of((me ^ distance) * share, share), share), :] = ref[...]
    two = two_ref[...]
    gram = pack(dot_of(two, two, (1, 1)))
    gram_ref[...] = gram
    for out_ref in outs:
        out_ref[count * (sum_ref.shape[0] // 2) :, :] = gram
    high = two.astype(jnp.bfloat16).astype(jnp.float32)
    both = jnp.concatenate([high, two - high], axis=0).T.astype(jnp.bfloat16)
    weight_ref[...] = jnp.concatenate([both, both], axis=0)

    def take(start):
        return split_ref[start * depth : (start + chunk) * depth, :]

    multiply(count, chunk, take, weight_ref, three_ref, outs, sum_ref)


def kept_kernel(
    count, chunk, tensor_ref, weight_ref, three_ref, gram_ref, out_ref, three_gram_ref, sum_ref, held_ref, sems
):
    me = lax.rem(lax.axis_index("gy"), 4)
    copies = load(tensor_ref, held_ref, sems, [4 * place + me for place in range(count)])
    piece = held_ref.shape[0] // len(copies)

    def take(start):
        if start % piece == 0:
            copies[start // piece].wait()
        return halves(held_ref[start : start + chunk])

    three = three_ref[...]
    three_gram_ref[...] = pack(dot_of(three, three, (0, 0)))
    multiply(count, chunk, take, weight_ref, three_ref, [out_ref], sum_ref)
    out_ref[count * (sum_ref.shape[0] // 2) :, :] = gram_ref[...]


def combine_kernel(half, count, *refs):
    parts, out_refs = refs[:-count], refs[-count:]
    me = lax.axis_index("gy") >> 2

    def total(rows):
        return functools.reduce(jnp.add, [part[rows, :] for part in parts])

    gram = total(slice(count * half, None))
    for distance, out_ref in enumerate(out_refs):
        out_ref[:half, :] = total(pl.ds(pl.multiple_of((me ^ distance) * half, half), half))
        out_ref[half:, :] = gram


def solve_kernel(*refs):
    *parts, three_gram_ref, out_ref, spread_ref = refs
    total = parts[0][...]
    for part in parts[1:]:
        total = total + part[...]
    half, (place, lanes) = out_ref.shape[0] // 2, three_gram_ref.shape
    gram = total[half:] * three_gram_ref[...]
    order = lanes // 2
    rows = lax.broadcasted_iota(jnp.int32, (order, lanes), 0)
    lane_ids = lax.broadcasted_iota(jnp.int32, (order, lanes), 1)
    joined = jnp.concatenate([pltpu.roll(gram, order, 1), gram], axis=0)
    joined = jnp.where(lane_ids < order, jnp.where(rows == lane_ids, 1.0, 0.0), joined)
    right = jnp.concatenate([total[:half], pltpu.roll(total[:half], order, 1)], axis=0)
    right = jnp.where(lax.broadcasted_iota(jnp.int32, right.shape, 1) < order, right, 0.0)

    tile = (8, lanes)
    bands = [joined[8 * g : 8 * g + 8] for g in range(order // 8)]
    places = lax.broadcasted_iota(jnp.int32, tile, 0)

    def lane(value, index):
        return jnp.broadcast_to(value[:, order + index : order + index + 1], tile)

    for own in range(len(bands)):
        base = 8 * own
        spot = 72 * own
        for p in range(8):
            spread_ref[spot + 8 * p : spot + 8 * p + 8, :] = lane(bands[own], base + p)
        spread_ref[spot + 64 : spot + 72, :] = bands[own]

        def spread(place):
            return jnp.broadcast_to(spread_ref[place : place + 1, :], tile)

        line = [spread(spot + 64 + q) for q in range(8)]
        entry = [[spread(spot + 8 * p + q) if p >= q else None for p in range(8)] for q in range(8)]
        inverse, done = [None] * 8, None

        def follow(band, column, q):
            scale = column[q] * inverse[q]
            band = band - scale * line[q]
            for p in range(q + 1, 8):
                column[p] = column[p] - scale * entry[q][p]
            return band

        near = bands[own + 1 : own + 2]
        column = [lane(band, base + q) for band in near for q in range(8)]
        for q in range(8):
            pivot = entry[q][q]
            inverse[q] = pltpu.reciprocal(pivot, approx=True)
            row = line[q] * lax.rsqrt(pivot)
            done = row if done is None else jnp.where(places == q, row, done)
            factor = [entry[q][p] * inverse[q] if p > q else None for p in range(8)]
            for p in range(q + 1, 8):
                entry[p][p] = entry[p][p] - (entry[q][p] * entry[q][p]) * inverse[q]
                for s in range(p + 1, 8):
                    entry[p][s] = entry[p][s] - factor[p] * entry[q][s]
                line[p] = line[p] - factor[p] * line[q]
            if near:
                bands[own + 1] = follow(bands[own + 1], column, q)
        bands[own] = done
        for h in range(own + 2, len(bands)):
            column = [lane(bands[h], base + q) for q in range(8)]
            for q in range(8):
                bands[h] = follow(bands[h], column, q)
    lower = jnp.concatenate(bands, axis=0)
    solved = dot_of(right, lower, (1, 1))
    out_ref[...] = dot_of(solved, lower, (1, 0))[:, :order]


def call(kernel, out_shape, args, flops, limit, scratch=(), specs=None):
    many = isinstance(out_shape, tuple)
    moved = sum(4 * a.size for a in args) + sum(4 * math.prod(o.shape) for o in (out_shape if many else (out_shape,)))
    return pl.pallas_call(
        kernel,
        out_shape=out_shape,
        in_specs=specs or [WHOLE] * len(args),
        out_specs=(WHOLE,) * len(out_shape) if many else WHOLE,
        scratch_shapes=scratch,
        compiler_params=pltpu.CompilerParams(vmem_limit_bytes=limit * 1024 * 1024),
        cost_estimate=pl.CostEstimate(flops=flops, bytes_accessed=moved, transcendentals=0),
    )(*args)


def body(tensor, factor_two, factor_three):
    groups, blocks = lax.axis_size("gx"), lax.axis_size("gy")
    rows, width, depth = tensor.shape
    rank = factor_three.shape[1]
    owned = rows // blocks
    half = owned // 2
    chunk = min(8, half)
    count = blocks // 4
    f32 = functools.partial(pltpu.VMEM, dtype=jnp.float32)
    packed = f32((rank // 2, 2 * rank))
    group = f32((count * half + rank // 2, 2 * rank))
    single = f32((half + rank // 2, 2 * rank))
    sums = f32((owned, 2 * rank))
    hbm = pl.BlockSpec(memory_space=pltpu.HBM)

    def held(size):
        return [f32((size * owned, depth, width)), pltpu.SemaphoreType.DMA((2 * size,))]

    mine = factor_two.T
    shares = [
        lax.ppermute(mine, "gx", [(i, i ^ distance) for i in range(groups)]) for distance in range(groups - 1, 0, -1)
    ]
    shares = [mine] + shares[::-1]
    tensor = pltpu.with_memory_space_constraint(jnp.transpose(tensor, (0, 2, 1)), pltpu.HBM)
    split = call(
        functools.partial(split_kernel, count, chunk),
        pltpu.VMEM((3 * count * owned * depth, 2 * width), jnp.bfloat16),
        (tensor,),
        10**9,
        12,
        held(3 * count),
        [hbm],
    )
    *sent, gram, weight = call(
        functools.partial(sent_kernel, groups, count, chunk),
        (group,) * len(ROUNDS) + (packed, pltpu.VMEM((2 * width, 2 * rank), jnp.bfloat16)),
        (split, factor_three, *shares),
        2 * 10**9,
        12,
        [f32((rank, width)), sums],
    )
    arrived = [
        lax.ppermute(value, "gy", [(i, i - i % 4 + table[i % 4]) for i in range(blocks)])
        for value, table in zip(sent, ROUNDS)
    ]
    total, three_gram = call(
        functools.partial(kept_kernel, count, chunk),
        (group, packed),
        (tensor, weight, factor_three, gram),
        2 * 10**9,
        12,
        [sums, *held(count)],
        [hbm, WHOLE, WHOLE, WHOLE],
    )
    kept, *sent = call(
        functools.partial(combine_kernel, half, count), (single,) * count, (total, *arrived), 10**6, 12
    )
    parts = [
        lax.ppermute(value, "gy", [(i, i ^ (4 * distance)) for i in range(blocks)])
        for distance, value in enumerate(sent, 1)
    ]
    return call(
        solve_kernel, jax.ShapeDtypeStruct((owned, rank), jnp.float32), (kept, *parts, three_gram), 10**8, 12, [f32((9 * rank, 2 * rank))]
    )


def solution(mesh):
    in_specs = (P("gx", "gy", None), P("gy", "gx"), P())
    out_specs = P(("gx", "gy"), None)
    return jax.shard_map(body, mesh=mesh, in_specs=in_specs, out_specs=out_specs, check_vma=False)
```

```python
import functools
import math

import jax
import jax.numpy as jnp
from jax import lax
from jax.experimental import pallas as pl
from jax.experimental.pallas import tpu as pltpu
from jax.sharding import PartitionSpec as P

HIGHEST = lax.Precision.HIGHEST
WHOLE = pl.BlockSpec(memory_space=pltpu.VMEM)


def dot_of(left, right, dims):
    return lax.dot_general(
        left, right, ((dims[:1], dims[1:]), ((), ())), precision=HIGHEST, preferred_element_type=jnp.float32
    )


def narrow_dot(left, right, dims):
    return lax.dot_general(left, right, ((dims[:1], dims[1:]), ((), ())), preferred_element_type=jnp.float32)


def parted(values):
    high = values.astype(jnp.bfloat16).astype(jnp.float32)
    return high, values - high


def pack(values):
    half = values.shape[0] // 2
    return jnp.concatenate([values[:half], values[half:]], axis=1)


ROUNDS = [(3, 2, 1, 0), (2, 3, 0, 1), (1, 0, 3, 2)]


def pick(table, place):
    value = table[0]
    for index, entry in enumerate(table):
        value = jnp.where(place == index, entry, value)
    return value


def load(tensor_ref, held_ref, sems, firsts):
    rows = held_ref.shape[0] // len(firsts)
    piece = held_ref.shape[0] // sems.shape[0]
    copies = []
    for place, first in enumerate(firsts):
        for start in range(0, rows, piece):
            copies.append(
                pltpu.make_async_copy(
                    tensor_ref.at[pl.ds(first * rows + start, piece)],
                    held_ref.at[pl.ds(place * rows + start, piece)],
                    sems.at[len(copies)],
                )
            )
    for copy in copies:
        copy.start()
    return copies


def halves(values):
    values = values.reshape(values.shape[0] * values.shape[1], values.shape[2])
    high = values.astype(jnp.bfloat16)
    low = (values - high.astype(jnp.float32)).astype(jnp.bfloat16)
    return jnp.concatenate([high, low], axis=1)


def split_kernel(count, chunk, tensor_ref, out_ref, held_ref, sems):
    me = lax.rem(lax.axis_index("gy"), 4)
    firsts = [4 * place + pick(table, me) for table in ROUNDS for place in range(count)]
    copies = load(tensor_ref, held_ref, sems, firsts)
    depth = held_ref.shape[1]
    piece = held_ref.shape[0] // len(copies)
    for index, copy in enumerate(copies):
        copy.wait()
        for start in range(index * piece, (index + 1) * piece, chunk):
            out_ref[start * depth : (start + chunk) * depth, :] = halves(held_ref[start : start + chunk])


def multiply(count, chunk, take, weight_ref, three_ref, outs, sum_ref):
    depth, rank = three_ref.shape
    rows = sum_ref.shape[0]
    half = rows // 2
    three = three_ref[...]
    three = jnp.concatenate([three, three], axis=1)[None]
    lower_half = lax.broadcasted_iota(jnp.int32, (half, 2 * rank), 1) < rank
    for block in range(count * len(outs)):
        for start in range(0, rows, chunk):
            product = jnp.dot(take(block * rows + start), weight_ref[...], preferred_element_type=jnp.float32)
            sum_ref[start : start + chunk, :] = jnp.sum(product.reshape(chunk, depth, 2 * rank) * three, axis=1)
        total = sum_ref[...]
        total = total + pltpu.roll(total, rank, 1)
        place = block % count * half
        outs[block // count][place : place + half, :] = jnp.where(lower_half, total[:half], total[half:])


def sent_kernel(groups, count, chunk, split_ref, three_ref, *refs):
    shares, refs = refs[:groups], refs[groups:]
    *outs, gram_ref, weight_ref, two_ref, sum_ref = refs
    me = lax.axis_index("gx")
    depth, share = three_ref.shape[0], shares[0].shape[0]
    for distance, ref in enumerate(shares):
        two_ref[pl.ds(pl.multiple_of((me ^ distance) * share, share), share), :] = ref[...]
    two = two_ref[...]
    high, low = parted(two)
    stacked = jnp.concatenate([high, low], axis=0)
    both = stacked.T.astype(jnp.bfloat16)
    weight_ref[...] = jnp.concatenate([both, both], axis=0)
    product = narrow_dot(stacked.astype(jnp.bfloat16), both, (1, 0))
    rank = two.shape[0]
    product = product[:rank] + product[rank:]
    gram = pack((product + pltpu.roll(product, rank, 1))[:, :rank])
    gram_ref[...] = gram
    for out_ref in outs:
        out_ref[count * (sum_ref.shape[0] // 2) :, :] = gram

    def take(start):
        return split_ref[start * depth : (start + chunk) * depth, :]

    multiply(count, chunk, take, weight_ref, three_ref, outs, sum_ref)


def kept_kernel(
    count, chunk, tensor_ref, weight_ref, three_ref, gram_ref, out_ref, three_gram_ref, sum_ref, held_ref, sems
):
    me = lax.rem(lax.axis_index("gy"), 4)
    copies = load(tensor_ref, held_ref, sems, [4 * place + me for place in range(count)])
    piece = held_ref.shape[0] // len(copies)

    def take(start):
        if start % piece == 0:
            copies[start // piece].wait()
        return halves(held_ref[start : start + chunk])

    three = three_ref[...]
    three_gram_ref[...] = pack(dot_of(three, three, (0, 0)))
    multiply(count, chunk, take, weight_ref, three_ref, [out_ref], sum_ref)
    out_ref[count * (sum_ref.shape[0] // 2) :, :] = gram_ref[...]


def combine_kernel(half, count, *refs):
    parts, out_refs = refs[:-count], refs[-count:]
    me = lax.axis_index("gy") >> 2

    def total(rows):
        return functools.reduce(jnp.add, [part[rows, :] for part in parts])

    gram = total(slice(count * half, None))
    for distance, out_ref in enumerate(out_refs):
        out_ref[:half, :] = total(pl.ds(pl.multiple_of((me ^ distance) * half, half), half))
        out_ref[half:, :] = gram


def solve_kernel(*refs):
    *parts, three_gram_ref, out_ref, spread_ref = refs
    total = parts[0][...]
    for part in parts[1:]:
        total = total + part[...]
    half, (place, lanes) = out_ref.shape[0] // 2, three_gram_ref.shape
    gram = total[half:] * three_gram_ref[...]
    order = lanes // 2
    rows = lax.broadcasted_iota(jnp.int32, (order, lanes), 0)
    lane_ids = lax.broadcasted_iota(jnp.int32, (order, lanes), 1)
    joined = jnp.concatenate([pltpu.roll(gram, order, 1), gram], axis=0)
    joined = jnp.where(lane_ids < order, jnp.where(rows == lane_ids, 1.0, 0.0), joined)
    right = jnp.concatenate([total[:half], pltpu.roll(total[:half], order, 1)], axis=0)
    right = jnp.where(lax.broadcasted_iota(jnp.int32, right.shape, 1) < order, right, 0.0)

    tile = (8, lanes)
    bands = [joined[8 * g : 8 * g + 8] for g in range(order // 8)]
    places = lax.broadcasted_iota(jnp.int32, tile, 0)

    def lane(value, index):
        return jnp.broadcast_to(value[:, order + index : order + index + 1], tile)

    for own in range(len(bands)):
        base = 8 * own
        spot = 72 * own
        for p in range(8):
            spread_ref[spot + 8 * p : spot + 8 * p + 8, :] = lane(bands[own], base + p)
        spread_ref[spot + 64 : spot + 72, :] = bands[own]

        def spread(place):
            return jnp.broadcast_to(spread_ref[place : place + 1, :], tile)

        line = [spread(spot + 64 + q) for q in range(8)]
        entry = [[spread(spot + 8 * p + q) if p >= q else None for p in range(8)] for q in range(8)]
        inverse, done = [None] * 8, None

        def follow(band, column, q):
            scale = column[q] * inverse[q]
            band = band - scale * line[q]
            for p in range(q + 1, 8):
                column[p] = column[p] - scale * entry[q][p]
            return band

        near = bands[own + 1 : own + 2]
        column = [lane(band, base + q) for band in near for q in range(8)]
        for q in range(8):
            pivot = entry[q][q]
            inverse[q] = pltpu.reciprocal(pivot, approx=True)
            row = line[q] * lax.rsqrt(pivot)
            done = row if done is None else jnp.where(places == q, row, done)
            factor = [entry[q][p] * inverse[q] if p > q else None for p in range(8)]
            for p in range(q + 1, 8):
                entry[p][p] = entry[p][p] - (entry[q][p] * entry[q][p]) * inverse[q]
                for s in range(p + 1, 8):
                    entry[p][s] = entry[p][s] - factor[p] * entry[q][s]
                line[p] = line[p] - factor[p] * line[q]
            if near:
                bands[own + 1] = follow(bands[own + 1], column, q)
        bands[own] = done
        for h in range(own + 2, len(bands)):
            column = [lane(bands[h], base + q) for q in range(8)]
            for q in range(8):
                bands[h] = follow(bands[h], column, q)
    left = lane_ids < order
    lower = jnp.where(left, jnp.concatenate(bands, axis=0), 0.0)
    lower_high, lower_low = parted(lower)
    right_high, right_low = parted(right)
    doubled = lower_high + pltpu.roll(lower_high, order, 1)
    factors = jnp.concatenate([doubled, lower_low], axis=1).astype(jnp.bfloat16)
    terms = jnp.concatenate([right_high + pltpu.roll(right_low, order, 1), right_high], axis=1).astype(jnp.bfloat16)
    solved = narrow_dot(terms, jnp.concatenate([factors, factors], axis=0), (1, 1))
    solved_high, solved_low = parted(solved)
    inside = lax.broadcasted_iota(jnp.int32, solved.shape, 1) < order
    terms = jnp.concatenate(
        [jnp.where(inside, solved_high, solved_low), jnp.where(inside, solved_high, 0.0)], axis=1
    ).astype(jnp.bfloat16)
    factors = jnp.concatenate([lower_high, lower_high, lower_low, lower_low], axis=0).astype(jnp.bfloat16)
    out_ref[...] = narrow_dot(terms, factors, (1, 0))[:, :order]


def call(kernel, out_shape, args, flops, limit, scratch=(), specs=None):
    many = isinstance(out_shape, tuple)
    moved = sum(4 * a.size for a in args) + sum(4 * math.prod(o.shape) for o in (out_shape if many else (out_shape,)))
    return pl.pallas_call(
        kernel,
        out_shape=out_shape,
        in_specs=specs or [WHOLE] * len(args),
        out_specs=(WHOLE,) * len(out_shape) if many else WHOLE,
        scratch_shapes=scratch,
        compiler_params=pltpu.CompilerParams(vmem_limit_bytes=limit * 1024 * 1024),
        cost_estimate=pl.CostEstimate(flops=flops, bytes_accessed=moved, transcendentals=0),
    )(*args)


def body(tensor, factor_two, factor_three):
    groups, blocks = lax.axis_size("gx"), lax.axis_size("gy")
    rows, width, depth = tensor.shape
    rank = factor_three.shape[1]
    owned = rows // blocks
    half = owned // 2
    chunk = min(16, half)
    count = blocks // 4
    f32 = functools.partial(pltpu.VMEM, dtype=jnp.float32)
    packed = f32((rank // 2, 2 * rank))
    group = f32((count * half + rank // 2, 2 * rank))
    single = f32((half + rank // 2, 2 * rank))
    sums = f32((owned, 2 * rank))
    hbm = pl.BlockSpec(memory_space=pltpu.HBM)

    def held(size):
        return [f32((size * owned, depth, width)), pltpu.SemaphoreType.DMA((2 * size,))]

    mine = factor_two.T
    shares = [
        lax.ppermute(mine, "gx", [(i, i ^ distance) for i in range(groups)]) for distance in range(groups - 1, 0, -1)
    ]
    shares = [mine] + shares[::-1]
    tensor = pltpu.with_memory_space_constraint(jnp.transpose(tensor, (0, 2, 1)), pltpu.HBM)
    split = call(
        functools.partial(split_kernel, count, chunk),
        pltpu.VMEM((3 * count * owned * depth, 2 * width), jnp.bfloat16),
        (tensor,),
        10**9,
        12,
        held(3 * count),
        [hbm],
    )
    *sent, gram, weight = call(
        functools.partial(sent_kernel, groups, count, chunk),
        (group,) * len(ROUNDS) + (packed, pltpu.VMEM((2 * width, 2 * rank), jnp.bfloat16)),
        (split, factor_three, *shares),
        2 * 10**9,
        12,
        [f32((rank, width)), sums],
    )
    arrived = [
        lax.ppermute(value, "gy", [(i, i - i % 4 + table[i % 4]) for i in range(blocks)])
        for value, table in zip(sent, ROUNDS)
    ]
    total, three_gram = call(
        functools.partial(kept_kernel, count, chunk),
        (group, packed),
        (tensor, weight, factor_three, gram),
        2 * 10**9,
        12,
        [sums, *held(count)],
        [hbm, WHOLE, WHOLE, WHOLE],
    )
    kept, *sent = call(
        functools.partial(combine_kernel, half, count), (single,) * count, (total, *arrived), 10**6, 12
    )
    parts = [
        lax.ppermute(value, "gy", [(i, i ^ (4 * distance)) for i in range(blocks)])
        for distance, value in enumerate(sent, 1)
    ]
    return call(
        solve_kernel, jax.ShapeDtypeStruct((owned, rank), jnp.float32), (kept, *parts, three_gram), 10**8, 12, [f32((9 * rank, 2 * rank))]
    )


def solution(mesh):
    in_specs = (P("gx", "gy", None), P("gy", "gx"), P())
    out_specs = P(("gx", "gy"), None)
    return jax.shard_map(body, mesh=mesh, in_specs=in_specs, out_specs=out_specs, check_vma=False)
```

```python
import functools
import math

import jax
import jax.numpy as jnp
from jax import lax
from jax.experimental import pallas as pl
from jax.experimental.pallas import tpu as pltpu
from jax.sharding import PartitionSpec as P

HIGHEST = lax.Precision.HIGHEST
WHOLE = pl.BlockSpec(memory_space=pltpu.VMEM)


def dot_of(left, right, dims):
    return lax.dot_general(
        left, right, ((dims[:1], dims[1:]), ((), ())), precision=HIGHEST, preferred_element_type=jnp.float32
    )


def narrow_dot(left, right, dims):
    return lax.dot_general(left, right, ((dims[:1], dims[1:]), ((), ())), preferred_element_type=jnp.float32)


def parted(values):
    high = values.astype(jnp.bfloat16).astype(jnp.float32)
    return high, values - high


def pack(values):
    half = values.shape[0] // 2
    return jnp.concatenate([values[:half], values[half:]], axis=1)


ROUNDS = [(3, 2, 1, 0), (2, 3, 0, 1), (1, 0, 3, 2)]


def pick(table, place):
    value = table[0]
    for index, entry in enumerate(table):
        value = jnp.where(place == index, entry, value)
    return value


def load(tensor_ref, held_ref, sems, firsts):
    rows = held_ref.shape[0] // len(firsts)
    piece = held_ref.shape[0] // sems.shape[0]
    copies = []
    for place, first in enumerate(firsts):
        for start in range(0, rows, piece):
            copies.append(
                pltpu.make_async_copy(
                    tensor_ref.at[pl.ds(first * rows + start, piece)],
                    held_ref.at[pl.ds(place * rows + start, piece)],
                    sems.at[len(copies)],
                )
            )
    for copy in copies:
        copy.start()
    return copies


def halves(values):
    values = values.reshape(values.shape[0] * values.shape[1], values.shape[2])
    high = values.astype(jnp.bfloat16)
    low = (values - high.astype(jnp.float32)).astype(jnp.bfloat16)
    return jnp.concatenate([high, low], axis=1)


def split_kernel(count, chunk, tensor_ref, out_ref, held_ref, sems):
    me = lax.rem(lax.axis_index("gy"), 4)
    firsts = [4 * place + pick(table, me) for table in ROUNDS for place in range(count)]
    copies = load(tensor_ref, held_ref, sems, firsts)
    depth = held_ref.shape[1]
    piece = held_ref.shape[0] // len(copies)
    for index, copy in enumerate(copies):
        copy.wait()
        for start in range(index * piece, (index + 1) * piece, chunk):
            out_ref[start * depth : (start + chunk) * depth, :] = halves(held_ref[start : start + chunk])


def multiply(count, chunk, take, weight_ref, three_ref, outs, sum_ref):
    depth, rank = three_ref.shape
    rows = sum_ref.shape[0]
    half = rows // 2
    three = three_ref[...]
    three = jnp.concatenate([three, three], axis=1)[None]
    lower_half = lax.broadcasted_iota(jnp.int32, (half, 2 * rank), 1) < rank
    for block in range(count * len(outs)):
        for start in range(0, rows, chunk):
            product = jnp.dot(take(block * rows + start), weight_ref[...], preferred_element_type=jnp.float32)
            sum_ref[start : start + chunk, :] = jnp.sum(product.reshape(chunk, depth, 2 * rank) * three, axis=1)
        total = sum_ref[...]
        total = total + pltpu.roll(total, rank, 1)
        place = block % count * half
        outs[block // count][place : place + half, :] = jnp.where(lower_half, total[:half], total[half:])


def sent_kernel(groups, count, chunk, split_ref, three_ref, *refs):
    shares, refs = refs[:groups], refs[groups:]
    *outs, gram_ref, weight_ref, two_ref, sum_ref = refs
    me = lax.axis_index("gx")
    depth, share = three_ref.shape[0], shares[0].shape[0]
    for distance, ref in enumerate(shares):
        two_ref[pl.ds(pl.multiple_of((me ^ distance) * share, share), share), :] = ref[...]
    two = two_ref[...]
    high, low = parted(two)
    stacked = jnp.concatenate([high, low], axis=0)
    both = stacked.T.astype(jnp.bfloat16)
    weight_ref[...] = jnp.concatenate([both, both], axis=0)
    product = narrow_dot(stacked.astype(jnp.bfloat16), both, (1, 0))
    rank = two.shape[0]
    product = product[:rank] + product[rank:]
    gram = pack((product + pltpu.roll(product, rank, 1))[:, :rank])
    gram_ref[...] = gram
    for out_ref in outs:
        out_ref[count * (sum_ref.shape[0] // 2) :, :] = gram

    def take(start):
        return split_ref[start * depth : (start + chunk) * depth, :]

    multiply(count, chunk, take, weight_ref, three_ref, outs, sum_ref)


def kept_kernel(
    count, chunk, tensor_ref, weight_ref, three_ref, gram_ref, out_ref, three_gram_ref, sum_ref, held_ref, sems
):
    me = lax.rem(lax.axis_index("gy"), 4)
    copies = load(tensor_ref, held_ref, sems, [4 * place + me for place in range(count)])
    piece = held_ref.shape[0] // len(copies)

    def take(start):
        if start % piece == 0:
            copies[start // piece].wait()
        return halves(held_ref[start : start + chunk])

    three = three_ref[...]
    three_gram_ref[...] = pack(dot_of(three, three, (0, 0)))
    multiply(count, chunk, take, weight_ref, three_ref, [out_ref], sum_ref)
    out_ref[count * (sum_ref.shape[0] // 2) :, :] = gram_ref[...]


def combine_kernel(half, count, *refs):
    parts, out_refs = refs[:-count], refs[-count:]
    me = lax.axis_index("gy") >> 2

    def total(rows):
        return functools.reduce(jnp.add, [part[rows, :] for part in parts])

    gram = total(slice(count * half, None))
    for distance, out_ref in enumerate(out_refs):
        out_ref[:half, :] = total(pl.ds(pl.multiple_of((me ^ distance) * half, half), half))
        out_ref[half:, :] = gram


def solve_kernel(*refs):
    *parts, three_gram_ref, out_ref, spread_ref = refs
    total = parts[0][...]
    for part in parts[1:]:
        total = total + part[...]
    half, (place, lanes) = out_ref.shape[0] // 2, three_gram_ref.shape
    gram = total[half:] * three_gram_ref[...]
    order = lanes // 2
    rows = lax.broadcasted_iota(jnp.int32, (order, lanes), 0)
    lane_ids = lax.broadcasted_iota(jnp.int32, (order, lanes), 1)
    joined = jnp.concatenate([pltpu.roll(gram, order, 1), gram], axis=0)
    joined = jnp.where(lane_ids < order, jnp.where(rows == lane_ids, 1.0, 0.0), joined)
    right = jnp.concatenate([total[:half], pltpu.roll(total[:half], order, 1)], axis=0)
    right = jnp.where(lax.broadcasted_iota(jnp.int32, right.shape, 1) < order, right, 0.0)

    tile = (8, lanes)
    bands = [joined[8 * g : 8 * g + 8] for g in range(order // 8)]
    places = lax.broadcasted_iota(jnp.int32, tile, 0)

    def lane(value, index):
        return jnp.broadcast_to(value[:, order + index : order + index + 1], tile)

    for own in range(len(bands)):
        base = 8 * own
        spot = 64 * own
        for p in range(8):
            spread_ref[spot + 8 * p : spot + 8 * p + 8, :] = lane(bands[own], base + p)

        def spread(place):
            return jnp.broadcast_to(spread_ref[place : place + 1, :], tile)

        line = [jnp.broadcast_to(bands[own][q : q + 1], tile) for q in range(8)]
        entry = [[spread(spot + 8 * p + q) if p >= q else None for p in range(8)] for q in range(8)]
        inverse, done = [None] * 8, None

        def follow(band, column, q):
            scale = column[q] * inverse[q]
            band = band - scale * line[q]
            for p in range(q + 1, 8):
                column[p] = column[p] - scale * entry[q][p]
            return band

        near = bands[own + 1 : own + 2]
        column = [lane(band, base + q) for band in near for q in range(8)]
        for q in range(8):
            pivot = entry[q][q]
            inverse[q] = pltpu.reciprocal(pivot, approx=True)
            row = line[q] * lax.rsqrt(pivot)
            done = row if done is None else jnp.where(places == q, row, done)
            factor = [entry[q][p] * inverse[q] if p > q else None for p in range(8)]
            for p in range(q + 1, 8):
                entry[p][p] = entry[p][p] - (entry[q][p] * entry[q][p]) * inverse[q]
                for s in range(p + 1, 8):
                    entry[p][s] = entry[p][s] - factor[p] * entry[q][s]
                line[p] = line[p] - factor[p] * line[q]
            if near:
                bands[own + 1] = follow(bands[own + 1], column, q)
        bands[own] = done
        for h in range(own + 2, len(bands)):
            column = [lane(bands[h], base + q) for q in range(8)]
            for q in range(8):
                bands[h] = follow(bands[h], column, q)
    lower = jnp.concatenate(bands, axis=0)
    solved = dot_of(right, lower, (1, 1))
    out_ref[...] = dot_of(solved, lower, (1, 0))[:, :order]


def call(kernel, out_shape, args, flops, limit, scratch=(), specs=None):
    many = isinstance(out_shape, tuple)
    moved = sum(4 * a.size for a in args) + sum(4 * math.prod(o.shape) for o in (out_shape if many else (out_shape,)))
    return pl.pallas_call(
        kernel,
        out_shape=out_shape,
        in_specs=specs or [WHOLE] * len(args),
        out_specs=(WHOLE,) * len(out_shape) if many else WHOLE,
        scratch_shapes=scratch,
        compiler_params=pltpu.CompilerParams(vmem_limit_bytes=limit * 1024 * 1024),
        cost_estimate=pl.CostEstimate(flops=flops, bytes_accessed=moved, transcendentals=0),
    )(*args)


def body(tensor, factor_two, factor_three):
    groups, blocks = lax.axis_size("gx"), lax.axis_size("gy")
    rows, width, depth = tensor.shape
    rank = factor_three.shape[1]
    owned = rows // blocks
    half = owned // 2
    chunk = min(16, half)
    count = blocks // 4
    f32 = functools.partial(pltpu.VMEM, dtype=jnp.float32)
    packed = f32((rank // 2, 2 * rank))
    group = f32((count * half + rank // 2, 2 * rank))
    single = f32((half + rank // 2, 2 * rank))
    sums = f32((owned, 2 * rank))
    hbm = pl.BlockSpec(memory_space=pltpu.HBM)

    def held(size):
        return [f32((size * owned, depth, width)), pltpu.SemaphoreType.DMA((2 * size,))]

    mine = factor_two.T
    shares = [
        lax.ppermute(mine, "gx", [(i, i ^ distance) for i in range(groups)]) for distance in range(groups - 1, 0, -1)
    ]
    shares = [mine] + shares[::-1]
    tensor = pltpu.with_memory_space_constraint(jnp.transpose(tensor, (0, 2, 1)), pltpu.HBM)
    split = call(
        functools.partial(split_kernel, count, chunk),
        pltpu.VMEM((3 * count * owned * depth, 2 * width), jnp.bfloat16),
        (tensor,),
        10**9,
        12,
        held(3 * count),
        [hbm],
    )
    *sent, gram, weight = call(
        functools.partial(sent_kernel, groups, count, chunk),
        (group,) * len(ROUNDS) + (packed, pltpu.VMEM((2 * width, 2 * rank), jnp.bfloat16)),
        (split, factor_three, *shares),
        2 * 10**9,
        12,
        [f32((rank, width)), sums],
    )
    arrived = [
        lax.ppermute(value, "gy", [(i, i - i % 4 + table[i % 4]) for i in range(blocks)])
        for value, table in zip(sent, ROUNDS)
    ]
    total, three_gram = call(
        functools.partial(kept_kernel, count, chunk),
        (group, packed),
        (tensor, weight, factor_three, gram),
        2 * 10**9,
        12,
        [sums, *held(count)],
        [hbm, WHOLE, WHOLE, WHOLE],
    )
    kept, *sent = call(
        functools.partial(combine_kernel, half, count), (single,) * count, (total, *arrived), 10**6, 12
    )
    parts = [
        lax.ppermute(value, "gy", [(i, i ^ (4 * distance)) for i in range(blocks)])
        for distance, value in enumerate(sent, 1)
    ]
    return call(
        solve_kernel, jax.ShapeDtypeStruct((owned, rank), jnp.float32), (kept, *parts, three_gram), 10**8, 12, [f32((8 * rank, 2 * rank))]
    )


def solution(mesh):
    in_specs = (P("gx", "gy", None), P("gy", "gx"), P())
    out_specs = P(("gx", "gy"), None)
    return jax.shard_map(body, mesh=mesh, in_specs=in_specs, out_specs=out_specs, check_vma=False)
```
